256 devices in a mesh: ctx: 32 (over y_lo, z, core), tp: 8 (over x, y_hi).
Axes of the slice: x: 4, y: 4 (y_hi: 2, y_lo: 2; y = y_hi * 2 + y_lo), z: 8, core: 2. Of those that a mesh axis runs over, the one named last changes fastest.
Arguments:
- query_act: bfloat16 [8192, 8192], P('ctx', 'tp'), may hold values from -6 to 6
- key_act: bfloat16 [8192, 1024], P('ctx', 'tp'), may hold values from -6 to 6
- value_act: bfloat16 [8192, 1024], P('ctx', 'tp'), may hold values from -6 to 6
- attn_out: bfloat16 [8192, 8192], P('ctx', 'tp'), may hold values from -6 to 6
- d_out: bfloat16 [8192, 8192], P('ctx', 'tp'), may hold values from -6 to 6
- log_norm: float32 [64, 8192], P('tp', 'ctx'), may hold values from 0 to 12
- span_order: int32 [64], replicated, may hold values from 0 to 63, as said below
- hidden: bfloat16 [8192, 5120], P('ctx'), may hold values from -0.0625 to 0.0625
- w_key: bfloat16 [5120, 1024], P(None, 'tp'), may hold values from -0.078125 to 0.078125
- w_value: bfloat16 [5120, 1024], P(None, 'tp'), may hold values from -0.078125 to 0.078125
Outputs:
- d_query: bfloat16 [8192, 8192], P('ctx', 'tp')
- d_key: bfloat16 [8192, 1024], P('ctx', 'tp')
- d_value: bfloat16 [8192, 1024], P('ctx', 'tp')
- grad_w_key: float32 [5120, 1024], P('ctx', 'tp')
- grad_w_value: float32 [5120, 1024], P('ctx', 'tp')
- d_hidden: bfloat16 [8192, 5120], P('ctx', 'tp')
The draws below stay inside these ranges and needn't reach their ends.
Inputs may be any that keep to these rules, and one draw needn't show every extreme that they name: `span_order`: storage spans 2 i and 2 i + 1 hold the sequence spans i and 63 - i, in either order.
All inputs are finite; a program needn't handle non-finite values.
Results may differ from the reference program's by a relative error of at most 0.015.
Values may be sent and summed in bfloat16 or wider, within the bound.
A program may use at most 64 MiB of HBM per device.

```python
import math
import jax
import jax.numpy as jnp
from jax import lax

D = 5120
HEADS = 64
KV_HEADS = 8
HEAD_DIM = 128
SPAN = 128
SPANS = 64
SEQ = 8192
N_TP = 8


def span_pairs(key):
    halves = SPANS // 2
    flips = jax.random.randint(jax.random.fold_in(key, 101), (halves,), 0, 2).astype(jnp.int32)
    lower = jnp.arange(halves, dtype=jnp.int32)
    upper = SPANS - 1 - lower
    first = jnp.where(flips == 1, upper, lower)
    second = jnp.where(flips == 1, lower, upper)
    return jnp.stack([first, second], axis=1).reshape(SPANS).astype(jnp.int32)


def draw_span_order(key, part):
    return span_pairs(key)


def draw_log_norm(key, part):
    order = span_pairs(key)
    key = jax.random.fold_in(key, 7)
    positions = (order[:, None] * SPAN + jnp.arange(SPAN, dtype=jnp.int32)[None, :]).reshape(SEQ)
    base = jnp.log(positions.astype(jnp.float32) + 1.0) + 0.5
    noise = jax.random.uniform(key, (HEADS, SEQ), jnp.float32, -0.5, 0.5)
    return base[None, :] + noise


def block_scale(rng, dims, pieces, low, top_value):
    factor_of = 1.0
    for axis_at, shards_of in pieces:
        heights = jax.random.uniform(jax.random.fold_in(jax.random.fold_in(rng, 6), axis_at), (shards_of,), jnp.float32, low / len(pieces), top_value / len(pieces))
        factor_of = factor_of * jnp.repeat(jnp.exp(heights), dims[axis_at] // shards_of).reshape((-1,) + (1,) * (len(dims) - 1 - axis_at))
    return factor_of


def centred(stream_key, dims, spread, most, split=(), held_as=jnp.bfloat16):
    result = spread * jax.random.normal(stream_key, dims, jnp.float32)
    if split:
        result = result * block_scale(stream_key, dims, split, -0.22, 0.18)
    return jnp.clip(result, -most, most).astype(held_as)


def setup_inputs(seed: int = 0) -> dict:
    keys = jax.random.split(jax.random.key(seed), 11)
    return {
        "query_act": centred(keys[0], (SEQ, HEADS * HEAD_DIM), 1.0, 6.0, ((0, 32), (1, 8))),
        "key_act": centred(keys[1], (SEQ, KV_HEADS * HEAD_DIM), 1.0, 6.0, ((0, 32), (1, 8))),
        "value_act": centred(keys[2], (SEQ, KV_HEADS * HEAD_DIM), 1.0, 6.0, ((0, 32), (1, 8))),
        "attn_out": centred(keys[3], (SEQ, HEADS * HEAD_DIM), 1.0, 6.0, ((0, 32), (1, 8))),
        "d_out": centred(keys[4], (SEQ, HEADS * HEAD_DIM), 1.0, 6.0, ((0, 32), (1, 8))),
        "log_norm": draw_log_norm(jax.random.fold_in(keys[10], 71), 0),
        "span_order": draw_span_order(jax.random.fold_in(keys[10], 71), 0),
        "hidden": centred(keys[7], (SEQ, D), SEQ ** -0.5, 0.0625, ((0, 32),)),
        "w_key": centred(keys[8], (D, KV_HEADS * HEAD_DIM), D ** -0.5, 0.078125, ((1, 8),)),
        "w_value": centred(keys[9], (D, KV_HEADS * HEAD_DIM), D ** -0.5, 0.078125, ((1, 8),)),
    }


def tile_grads(q_tile, grad_tile, norm_tile, delta_tile, key_tile, value_tile, q_pos, k_pos, score_scale):
    q_wide = q_tile.astype(jnp.float32)
    grad_wide = grad_tile.astype(jnp.float32)
    key_wide = key_tile.astype(jnp.float32)
    value_wide = value_tile.astype(jnp.float32)
    scores = jnp.einsum('qgd,kd->gqk', q_wide, key_wide) * score_scale
    visible = k_pos[None, None, :] <= q_pos[None, :, None]
    probs = jnp.where(visible, jnp.exp(scores - norm_tile[:, :, None]), jnp.float32(0.0))
    dprobs = jnp.einsum('qgd,kd->gqk', grad_wide, value_wide)
    dscores = probs * (dprobs - delta_tile[:, :, None])
    probs_low = lax.optimization_barrier(probs.astype(jnp.bfloat16)).astype(jnp.float32)
    dscores_low = lax.optimization_barrier(dscores.astype(jnp.bfloat16)).astype(jnp.float32)
    d_vals = jnp.einsum('gqk,qgd->kd', probs_low, grad_wide)
    d_keys = jnp.einsum('gqk,qgd->kd', dscores_low, q_wide) * score_scale
    d_quer = jnp.einsum('gqk,kd->qgd', dscores_low, key_wide) * score_scale
    return (d_quer, d_keys, d_vals)

def reference(query_act, key_act, value_act, attn_out, d_out, log_norm, span_order, hidden, w_key, w_value):
    seq_len = query_act.shape[0]
    spans_all = span_order.shape[0]
    span_len = seq_len // spans_all
    group_size = HEADS // KV_HEADS
    score_scale = 1.0 / math.sqrt(HEAD_DIM)
    block_len = math.gcd(seq_len, 512)
    block_count = seq_len // block_len
    inverse = jnp.argsort(span_order).astype(jnp.int32)

    def to_pos(array):
        return jnp.take(array.reshape(spans_all, span_len, -1), inverse, axis=0).reshape(seq_len, -1)

    def to_store(array):
        return jnp.take(array.reshape(spans_all, span_len, -1), span_order.astype(jnp.int32), axis=0).reshape(seq_len, -1)
    q_pos_all = to_pos(query_act).reshape(seq_len, KV_HEADS, group_size, HEAD_DIM)
    grad_pos = to_pos(d_out).reshape(seq_len, KV_HEADS, group_size, HEAD_DIM)
    out_pos = to_pos(attn_out).reshape(seq_len, KV_HEADS, group_size, HEAD_DIM)
    delta = lax.optimization_barrier(jnp.sum(grad_pos.astype(jnp.float32) * out_pos.astype(jnp.float32), axis=-1))
    norms = to_pos(log_norm.T).reshape(seq_len, KV_HEADS, group_size)
    keys_pos = to_pos(key_act).reshape(seq_len, KV_HEADS, HEAD_DIM)
    values_pos = to_pos(value_act).reshape(seq_len, KV_HEADS, HEAD_DIM)
    packed = (jnp.transpose(q_pos_all, (1, 0, 2, 3)), jnp.transpose(grad_pos, (1, 0, 2, 3)), jnp.transpose(norms, (1, 2, 0)), jnp.transpose(delta, (1, 2, 0)), jnp.transpose(keys_pos, (1, 0, 2)), jnp.transpose(values_pos, (1, 0, 2)))

    def head_grads(items):
        q_head, grad_head, norm_head, delta_head, key_head, value_head = items

        def query_block(block_idx, state):
            dq_all, dk_all, dv_all = state
            q_start = (block_idx * block_len).astype(jnp.int32)
            q_tile = lax.dynamic_slice_in_dim(q_head, q_start, block_len, 0)
            grad_tile = lax.dynamic_slice_in_dim(grad_head, q_start, block_len, 0)
            norm_tile = lax.dynamic_slice_in_dim(norm_head, q_start, block_len, 1)
            delta_tile = lax.dynamic_slice_in_dim(delta_head, q_start, block_len, 1)
            q_pos = q_start + jnp.arange(block_len, dtype=jnp.int32)

            def key_block(key_idx, inner):
                dq_tile, dk_run, dv_run = inner
                k_start = (key_idx * block_len).astype(jnp.int32)
                key_tile = lax.dynamic_slice_in_dim(key_head, k_start, block_len, 0)
                value_tile = lax.dynamic_slice_in_dim(value_head, k_start, block_len, 0)
                k_pos = k_start + jnp.arange(block_len, dtype=jnp.int32)
                d_quer, d_keys, d_vals = tile_grads(q_tile, grad_tile, norm_tile, delta_tile, key_tile, value_tile, q_pos, k_pos, score_scale)
                dk_run = lax.dynamic_update_slice_in_dim(dk_run, lax.dynamic_slice_in_dim(dk_run, k_start, block_len, 0) + d_keys, k_start, 0)
                dv_run = lax.dynamic_update_slice_in_dim(dv_run, lax.dynamic_slice_in_dim(dv_run, k_start, block_len, 0) + d_vals, k_start, 0)
                return (dq_tile + d_quer, dk_run, dv_run)
            dq_zero = jnp.zeros((block_len, group_size, HEAD_DIM), jnp.float32)
            dq_tile, dk_all, dv_all = lax.fori_loop(0, block_idx + 1, key_block, (dq_zero, dk_all, dv_all))
            dq_all = lax.dynamic_update_slice_in_dim(dq_all, dq_tile, q_start, 0)
            return (dq_all, dk_all, dv_all)
        start_state = (jnp.zeros((seq_len, group_size, HEAD_DIM), jnp.float32), jnp.zeros((seq_len, HEAD_DIM), jnp.float32), jnp.zeros((seq_len, HEAD_DIM), jnp.float32))
        return lax.fori_loop(0, block_count, query_block, start_state)
    dq_heads, dk_heads, dv_heads = lax.map(head_grads, packed)
    d_query = to_store(jnp.transpose(dq_heads, (1, 0, 2, 3)).reshape(seq_len, -1).astype(jnp.bfloat16))
    d_key = to_store(jnp.transpose(dk_heads, (1, 0, 2)).reshape(seq_len, -1).astype(jnp.bfloat16))
    d_value = to_store(jnp.transpose(dv_heads, (1, 0, 2)).reshape(seq_len, -1).astype(jnp.bfloat16))
    grad_w_key = jnp.dot(hidden.T, d_key, preferred_element_type=jnp.float32)
    grad_w_value = jnp.dot(hidden.T, d_value, preferred_element_type=jnp.float32)
    kv_cols = KV_HEADS * HEAD_DIM // N_TP
    summed = jnp.zeros((seq_len, hidden.shape[1]), jnp.float32)
    for group_idx in range(N_TP):
        lo_col = group_idx * kv_cols
        partial_part = jnp.dot(d_key[:, lo_col:lo_col + kv_cols], w_key[:, lo_col:lo_col + kv_cols].T, preferred_element_type=jnp.float32)
        partial_part = partial_part + jnp.dot(d_value[:, lo_col:lo_col + kv_cols], w_value[:, lo_col:lo_col + kv_cols].T, preferred_element_type=jnp.float32)
        summed = summed + lax.optimization_barrier(partial_part.astype(jnp.bfloat16)).astype(jnp.float32)
    d_hidden = summed.astype(jnp.bfloat16)
    return (d_query, d_key, d_value, grad_w_key, grad_w_value, d_hidden)
```

```python
import functools
import math

import jax
import jax.numpy as jnp
from jax import lax
from jax.experimental import pallas as pl
from jax.experimental.pallas import tpu as pltpu
from jax.sharding import PartitionSpec as P

BF = jnp.bfloat16
F32 = jnp.float32
MESH = pl.DeviceIdType.MESH
SCALE = 1.0 / math.sqrt(128)
LOG2E = math.log2(math.e)
NT = (((1,), (1,)), ((), ()))
TN = (((0,), (0,)), ((), ()))
SPAN = 128
TP = 8
NZ = 8
FEAT = 640
HALF_FEAT = 320
WROWS = 160

dot = functools.partial(lax.dot_general, preferred_element_type=F32)


def mm(a, b):
    return jnp.dot(a, b, preferred_element_type=F32)


def place():
    i = lax.axis_index("ctx")
    core = i % 2
    z = (i // 2) % NZ
    y = i // 16
    rank = jnp.where(core == 0, z, 7 - z)
    return i, core, z, y, rank


def ctx_of(y, z, core):
    return y * 16 + z * 2 + core


def remote(src, dst, send, recv, **where):
    return pltpu.make_async_remote_copy(
        src_ref=src, dst_ref=dst, send_sem=send, recv_sem=recv, device_id=where, device_id_type=MESH
    )


def neighbours(core, z, y):
    up = (z + 1) % NZ
    down = (z + NZ - 1) % NZ
    nxt = ctx_of(y, jnp.where(core == 0, up, down), core)
    prv = ctx_of(y, jnp.where(core == 0, down, up), core)
    return nxt, prv, ctx_of(1 - y, z, core), ctx_of(y, z, 1 - core)


def attention_kernel(
    swapped, q_in, k_in, v_in, o_in, d_in, ln_in, wk, wv,
    dq_out, dk_out, dv_out, wbuf,
    qb, db, ob, lnc, lnb, deb, dqa, kv, acc, sin, sout, dqs, dqr, ys, yr,
    xsend, xrecv, zsend, zrecv, ysend, yrecv, ssend, srecv, wsend, wrecv, fsend, frecv, dsem, lsem,
):
    i, core, z, y, rank = place()
    tp = lax.axis_index("tp")
    other = 1 - core
    nxt, prv, ypart, mate = neighbours(core, z, y)
    odd = rank % 2
    pair = rank // 2
    chip = y * NZ + z

    barrier = pltpu.get_barrier_semaphore()
    for dev in (nxt, prv, ypart, mate):
        pl.semaphore_signal(barrier, inc=1, device_id={"ctx": dev}, device_id_type=MESH)
    for step in range(1, TP):
        pl.semaphore_signal(
            barrier, inc=1, device_id={"tp": (tp + step) % TP}, device_id_type=MESH
        )

    flip_wide = jnp.concatenate([swapped[...]] * 16, axis=0)
    flip16 = flip_wide.astype(BF) > 0.5

    def canon(first, second, hl):
        return jnp.where(flip16, second, first) if hl == 0 else jnp.where(flip16, first, second)

    for hl in range(2):
        kv[y, rank, hl] = canon(k_in[:SPAN, :], k_in[SPAN:, :], hl)
        kv[y, rank, 2 + hl] = canon(v_in[:SPAN, :], v_in[SPAN:, :], hl)
    pl.semaphore_wait(barrier, 4 + TP - 1)

    def gather_z(s):
        block = kv.at[y, (rank - s + NZ) % NZ]
        return remote(block, block, zsend.at[s], zrecv.at[s + 1], ctx=nxt)

    def gather_y(s):
        block = kv.at[y, (rank - s + NZ) % NZ]
        return remote(block, block, ysend.at[s], yrecv.at[s], ctx=ypart)

    gather_z(0).start()
    gather_y(0).start()

    for hl in range(2):
        for h in range(8):
            cols = slice(h * 128, (h + 1) * 128)
            for full, here in ((qb, q_in), (db, d_in), (ob, o_in)):
                full[core, hl, cols, :] = canon(here[:SPAN, cols], here[SPAN:, cols], hl)
    both = ln_in[...] * LOG2E
    flip8 = swapped[...] > 0.5
    lnc[core, 0] = jnp.where(flip8, both[:, SPAN:], both[:, :SPAN])
    lnc[core, 1] = jnp.where(flip8, both[:, :SPAN], both[:, SPAN:])
    swaps = [
        remote(ref.at[core], ref.at[core], xsend.at[n], xrecv.at[n], ctx=mate)
        for n, ref in enumerate((qb, db, ob, lnc))
    ]
    for swap in swaps:
        swap.start()

    def zero(n, _):
        for part in range(4):
            acc[n // NZ, n % NZ, part] = jnp.zeros((128, 128), F32)
        return 0

    lax.fori_loop(0, 2 * NZ, zero, 0)
    dqa[...] = jnp.zeros_like(dqa)

    ones = jnp.ones((128, 128), BF)
    head_of = lax.broadcasted_iota(jnp.int32, (32, 1024), 1) // 128
    pick = (lax.broadcasted_iota(jnp.int32, (32, 1024), 0) % 8 == head_of).astype(F32).astype(BF)

    def row_terms(slot):
        for hl in range(2):
            prod = db[slot, hl].astype(F32) * ob[slot, hl].astype(F32)
            high = prod.astype(BF)
            low = (prod - high.astype(F32)).astype(BF)
            deb[slot, hl] = mm(high, ones) + mm(low, ones)
            norm = lnc[slot, hl]
            p1 = norm.astype(BF)
            rest = norm - p1.astype(F32)
            p2 = rest.astype(BF)
            rest = rest - p2.astype(F32)
            p3 = rest.astype(BF)
            parts = jnp.concatenate(
                [p1.astype(F32), p2.astype(F32), p3.astype(F32), jnp.zeros((8, 128), F32)], axis=0
            ).astype(BF)
            wide = dot(parts, pick, TN)
            for h in range(8):
                lnb[slot, hl, h * 128 : (h + 1) * 128, :] = wide[:, h * 128 : (h + 1) * 128]

    row_terms(core)
    for swap in swaps:
        swap.wait()
    row_terms(other)

    def pump(s):
        remote(
            kv.at[y, (rank - s + NZ) % NZ], kv.at[y, (rank - s + NZ) % NZ],
            zsend.at[0], zrecv.at[s], ctx=nxt,
        ).wait_recv()
        gather_y(s).start()

        @pl.when(s < NZ - 1)
        def _():
            gather_z(s).start()

    pump(1)
    pump(2)

    def z_of(rk):
        return jnp.where(core == 0, rk, 7 - rk)

    def unit(yp, w, hk, hq, masked):
        ra = 2 * w
        rb = 2 * w + 1
        k = jnp.concatenate([kv[yp, ra, hk], kv[yp, rb, hk]], axis=0)
        v = jnp.concatenate([kv[yp, ra, 2 + hk], kv[yp, rb, 2 + hk]], axis=0)
        gk = None
        gv = None
        for slot in range(2):
            q = qb[slot, hq]
            d = db[slot, hq]
            ln = lnb[slot, hq]
            de = deb[slot, hq]
            scores = dot(q, k, NT)
            dp = dot(d, v, NT)
            prob = jnp.exp2(scores * (SCALE * LOG2E) - jnp.concatenate([ln, ln], axis=1))
            if masked:
                qi = 2 * chip + slot
                qspan = jnp.where(hq == 0, qi, 63 - qi)
                shape = (1024, 128)
                gap = (
                    lax.broadcasted_iota(jnp.int32, shape, 0) % SPAN
                    - lax.broadcasted_iota(jnp.int32, shape, 1)
                )
                seen = []
                for rk in (ra, rb):
                    ki = 2 * (yp * NZ + z_of(rk)) + core
                    kspan = jnp.where(hk == 0, ki, 63 - ki)
                    seen.append(gap >= (kspan - qspan) * SPAN)
                prob = jnp.concatenate(
                    [
                        jnp.where(seen[0], prob[:, :128], 0.0),
                        jnp.where(seen[1], prob[:, 128:], 0.0),
                    ],
                    axis=1,
                )
            ds = (prob * (dp - jnp.concatenate([de, de], axis=1))).astype(BF)
            pr = prob.astype(BF)
            dqa[slot, hq] += mm(ds, k)
            gk = dot(q, ds, TN) if gk is None else gk + dot(q, ds, TN)
            gv = dot(d, pr, TN) if gv is None else gv + dot(d, pr, TN)
        acc[yp, ra, hk] += gk[:, :128]
        acc[yp, rb, hk] += gk[:, 128:]
        acc[yp, ra, 2 + hk] += gv[:, :128]
        acc[yp, rb, 2 + hk] += gv[:, 128:]

    def where_at(x):
        n = x // 2
        w = (pair - n - (1 - odd) + 8) % 4
        yp = (y + x) % 2
        return w, yp

    def sum_copy(yp, rk):
        return remote(sout.at[yp, rk], sin.at[yp, rk], ssend.at[yp, rk], srecv.at[yp, rk], ctx=nxt)

    def pass_sums(x):
        w, yp = where_at(x)
        for rk in (2 * w + 1, 2 * w):
            s = (rank - rk + NZ) % NZ

            @pl.when(s == 1)
            def _():
                sout[yp, rk] = acc[yp, rk].astype(BF)

            @pl.when(s > 1)
            def _():
                sum_copy(yp, rk).wait_recv()
                sout[yp, rk] = (acc[yp, rk] + sin[yp, rk].astype(F32)).astype(BF)

            @pl.when(s > 0)
            def _():
                sum_copy(yp, rk).start()

    def weight_copies(step):
        peer = (tp + step) % TP
        out = []
        for n, ref in enumerate((wk, wv)):
            rows = pl.ds(pl.multiple_of(peer * FEAT + core * HALF_FEAT, 64), HALF_FEAT)
            mine = pl.ds(pl.multiple_of(core * HALF_FEAT, 64), HALF_FEAT)
            out.append(
                remote(
                    ref.at[rows, :], wbuf.at[tp, n, mine, :],
                    wsend.at[step, n], wrecv.at[step, n], tp=peer,
                )
            )
        return out

    def weight_forwards(step):
        giver = (tp + TP - step) % TP
        out = []
        for n in range(2):
            mine = pl.ds(pl.multiple_of(core * HALF_FEAT, 64), HALF_FEAT)
            block = wbuf.at[giver, n, mine, :]
            out.append(remote(block, block, fsend.at[step, n], frecv.at[step, n], ctx=mate))
        return out

    def half_step(x, _):
        w, yp = where_at(x)
        g = x % 2

        @pl.when(g == 1)
        def _():
            for rk in (2 * w + 1, 2 * w):
                s = (rank - rk + NZ) % NZ
                block = kv.at[yp, rk]
                remote(block, block, ysend.at[0], yrecv.at[s], ctx=ypart).wait_recv()

        @pl.when(x > 0)
        def _():
            for copy in weight_copies(x):
                copy.start()

        unit(yp, w, 0, 1, False)
        own = jnp.logical_and(g == 0, w == pair)

        @pl.when(own)
        def _():
            def masked_unit(hl, _):
                unit(yp, w, hl, hl, True)
                return 0

            lax.fori_loop(0, 2, masked_unit, 0)

        @pl.when(jnp.logical_not(own))
        def _():
            hl = jnp.where(yp * NZ + z_of(2 * w) < chip, 0, 1)
            unit(yp, w, hl, hl, False)

        @pl.when(x < 5)
        def _():
            pump(x + 3)

        @pl.when(x > 1)
        def _():
            for copy in weight_copies(x - 1):
                copy.wait_recv()
            for copy in weight_forwards(x - 1):
                copy.start()

        ready = x - (1 - odd)

        @pl.when(ready >= 0)
        def _():
            pass_sums(ready)

        return 0

    lax.fori_loop(0, 8, half_step, 0)

    dqs[...] = (dqa[other] * SCALE).astype(BF)
    dq_copy = remote(dqs, dqr, dsem.at[0], dsem.at[1], ctx=mate)
    dq_copy.start()

    @pl.when(odd == 0)
    def _():
        pass_sums(7)

    for copy in weight_copies(TP - 1):
        copy.wait_recv()
    for copy in weight_forwards(TP - 1):
        copy.start()

    sum_copy(1 - y, rank).wait_recv()
    ys[...] = (acc[1 - y, rank] + sin[1 - y, rank].astype(F32)).astype(BF)
    y_copy = remote(ys, yr, dsem.at[2], dsem.at[3], ctx=ypart)
    y_copy.start()

    dq_copy.wait()
    for h in range(8):
        cols = slice(h * 128, (h + 1) * 128)
        low = (dqa[core, 0, cols, :] * SCALE + dqr[0, cols, :].astype(F32)).astype(BF)
        high = (dqa[core, 1, cols, :] * SCALE + dqr[1, cols, :].astype(F32)).astype(BF)
        dq_out[0:SPAN, cols] = jnp.where(flip16, high, low)
        dq_out[SPAN:, cols] = jnp.where(flip16, low, high)

    sum_copy(y, rank).wait_recv()
    y_copy.wait()
    total = acc[y, rank] + sin[y, rank].astype(F32) + yr[...].astype(F32)
    for out, at, factor in ((dk_out, 0, SCALE), (dv_out, 2, 1.0)):
        low = (total[at] * factor).T.astype(BF)
        high = (total[at + 1] * factor).T.astype(BF)
        out[0:SPAN, :] = jnp.where(flip16, high, low)
        out[SPAN:, :] = jnp.where(flip16, low, high)

    def drain(s, _):
        gather_y(s).wait_send()

        @pl.when(s < NZ - 1)
        def _():
            gather_z(s).wait_send()

        @pl.when(s > 0)
        def _():
            for copy in weight_copies(s):
                copy.wait_send()
            for copy in weight_forwards(s):
                copy.wait()
            for yp in range(2):
                sum_copy(yp, (rank - s + NZ) % NZ).wait_send()

        return 0

    lax.fori_loop(0, NZ, drain, 0)


def attention(swapped, q, k, v, o, d, ln, wk, wv):
    vmem = pl.BlockSpec(memory_space=pltpu.VMEM)
    anyw = pl.BlockSpec(memory_space=pl.ANY)
    dma = pltpu.SemaphoreType.DMA
    sds = jax.ShapeDtypeStruct
    rows = (2, 2, 1024, 128)
    block = (4, 128, 128)
    return pl.pallas_call(
        attention_kernel,
        out_shape=[
            sds((256, 1024), BF),
            sds((256, 128), BF),
            sds((256, 128), BF),
            sds((TP, 2, FEAT, 128), BF),
        ],
        in_specs=[vmem] * 7 + [anyw] * 2,
        out_specs=[vmem, vmem, vmem, anyw],
        scratch_shapes=[
            pltpu.VMEM(rows, BF),
            pltpu.VMEM(rows, BF),
            pltpu.VMEM(rows, BF),
            pltpu.VMEM((2, 2, 8, 128), F32),
            pltpu.VMEM(rows, F32),
            pltpu.VMEM(rows, F32),
            pltpu.VMEM(rows, F32),
            pltpu.VMEM((2, NZ) + block, BF),
            pltpu.VMEM((2, NZ) + block, F32),
            pltpu.VMEM((2, NZ) + block, BF),
            pltpu.VMEM((2, NZ) + block, BF),
            pltpu.VMEM((2, 1024, 128), BF),
            pltpu.VMEM((2, 1024, 128), BF),
            pltpu.VMEM(block, BF),
            pltpu.VMEM(block, BF),
            dma((4,)),
            dma((4,)),
            dma((NZ,)),
            dma((NZ,)),
            dma((NZ,)),
            dma((NZ,)),
            dma((2, NZ)),
            dma((2, NZ)),
            dma((TP, 2)),
            dma((TP, 2)),
            dma((TP, 2)),
            dma((TP, 2)),
            dma((4,)),
            dma((1,)),
        ],
        compiler_params=pltpu.CompilerParams(
            collective_id=0, has_side_effects=True, vmem_limit_bytes=48 * 2**20
        ),
        cost_estimate=pl.CostEstimate(
            flops=11 * 10**9, bytes_accessed=10**7, transcendentals=9 * 10**6
        ),
    )(swapped, q, k, v, o, d, ln, wk, wv)


def project_kernel(
    dk, dv, hid, wbuf, wko, wvo,
    gk_out, gv_out, dh_out,
    dkv, gathered, part, cs, cr, rin, rout, ys, yr,
    gsend, grecv, csem, rsend, rrecv, ysem,
):
    i, core, z, y, rank = place()
    tp = lax.axis_index("tp")
    other = 1 - core
    nxt, prv, ypart, mate = neighbours(core, z, y)

    barrier = pltpu.get_barrier_semaphore()
    for dev in (nxt, prv, ypart, mate):
        pl.semaphore_signal(barrier, inc=1, device_id={"ctx": dev}, device_id_type=MESH)
    for step in range(1, TP):
        pl.semaphore_signal(
            barrier, inc=1, device_id={"tp": (tp + step) % TP}, device_id_type=MESH
        )
    dkv[:, 0:128] = dk[...]
    dkv[:, 128:256] = dv[...]
    pl.semaphore_wait(barrier, 4 + TP - 1)

    def spread(step):
        return remote(
            dkv, gathered.at[tp], gsend.at[step], grecv.at[step], tp=(tp + step) % TP
        )

    for step in range(1, TP):
        spread(step).start()

    mine = dkv[...]
    for n in range(8):
        part[pl.ds(n * 640, 640), :] = dot(hid[:, n * 640 : (n + 1) * 640], mine, TN)

    def rows_of(c, k):
        return pl.ds(pl.multiple_of((c * 2 + k) * WROWS, 32), WROWS)

    def fill(c, _):
        cs[c] = part[rows_of(c, other), :].astype(BF)
        return 0

    lax.fori_loop(0, 16, fill, 0)
    swap = remote(cs, cr, csem.at[0], csem.at[1], ctx=mate)
    swap.start()

    total = mm(mine[:, :128], wko[...].T) + mm(mine[:, 128:], wvo[...].T)
    dh_out[...] = total.astype(BF)
    swap.wait()

    def z_of(rk):
        return jnp.where(core == 0, rk, 7 - rk)

    def own_part(yp, rk):
        c = yp * NZ + z_of(rk)
        return part[rows_of(c, core), :] + cr[c].astype(F32)

    def chain(yp, s):
        rk = (rank - s + NZ) % NZ
        return remote(rout.at[yp, s], rin.at[yp, s + 1], rsend.at[yp, s], rrecv.at[yp, s + 1], ctx=nxt)

    for yp in range(2):
        rout[yp, 1] = own_part(yp, (rank + 7) % NZ).astype(BF)
        chain(yp, 1).start()

    def hop(s, _):
        for yp in range(2):
            chain(yp, s - 1).wait_recv()
            rout[yp, s] = (own_part(yp, (rank - s + NZ) % NZ) + rin[yp, s].astype(F32)).astype(BF)
            chain(yp, s).start()
        return 0

    lax.fori_loop(2, NZ, hop, 0)
    for yp in range(2):
        chain(yp, NZ - 1).wait_recv()
    ys[...] = (own_part(1 - y, rank) + rin[1 - y, NZ].astype(F32)).astype(BF)
    y_copy = remote(ys, yr, ysem.at[0], ysem.at[1], ctx=ypart)
    y_copy.start()
    for step in range(1, TP):
        spread(step).wait_recv()

    acc = jnp.zeros((256, FEAT), F32)
    for step in range(1, TP):
        giver = (tp + TP - step) % TP
        got = gathered[giver]
        acc += dot(got[:, :128], wbuf[giver, 0], NT) + dot(got[:, 128:], wbuf[giver, 1], NT)
    dh_out[...] = (acc + total).astype(BF)

    y_copy.wait()
    final = own_part(y, rank) + rin[y, NZ].astype(F32) + yr[...].astype(F32)
    gk_out[...] = final[:, :128]
    gv_out[...] = final[:, 128:]
    for step in range(1, TP):
        spread(step).wait_send()

    def drain(s, _):
        for yp in range(2):
            chain(yp, s).wait_send()
        return 0

    lax.fori_loop(1, NZ, drain, 0)


def project(dk, dv, hid, wbuf, wko, wvo):
    vmem = pl.BlockSpec(memory_space=pltpu.VMEM)
    dma = pltpu.SemaphoreType.DMA
    sds = jax.ShapeDtypeStruct
    piece = (WROWS, 256)
    return pl.pallas_call(
        project_kernel,
        out_shape=[sds((WROWS, 128), F32), sds((WROWS, 128), F32), sds((256, FEAT), BF)],
        in_specs=[vmem] * 6,
        out_specs=[vmem] * 3,
        scratch_shapes=[
            pltpu.VMEM((256, 256), BF),
            pltpu.VMEM((TP, 256, 256), BF),
            pltpu.VMEM((5120, 256), F32),
            pltpu.VMEM((16,) + piece, BF),
            pltpu.VMEM((16,) + piece, BF),
            pltpu.VMEM((2, NZ + 1) + piece, BF),
            pltpu.VMEM((2, NZ) + piece, BF),
            pltpu.VMEM(piece, BF),
            pltpu.VMEM(piece, BF),
            dma((TP,)),
            dma((TP,)),
            dma((2,)),
            dma((2, NZ)),
            dma((2, NZ + 1)),
            dma((2,)),
        ],
        compiler_params=pltpu.CompilerParams(
            collective_id=1, has_side_effects=True, vmem_limit_bytes=48 * 2**20
        ),
        cost_estimate=pl.CostEstimate(flops=2 * 10**9, bytes_accessed=10**7, transcendentals=0),
    )(dk, dv, hid, wbuf, wko, wvo)


def shards(q, k, v, o, d, ln, order, hidden, wk, wv):
    i = lax.axis_index("ctx")
    swapped = jnp.full((8, 128), (order[2 * i] != i).astype(F32))
    dq, dk, dv, wbuf = attention(swapped, q, k, v, o, d, ln, wk, wv)
    tp = lax.axis_index("tp")
    wko = lax.dynamic_slice_in_dim(wk, tp * FEAT, FEAT, 0)
    wvo = lax.dynamic_slice_in_dim(wv, tp * FEAT, FEAT, 0)
    gk, gv, dh = project(dk, dv, hidden, wbuf, wko, wvo)
    return dq, dk, dv, gk, gv, dh


def solution(mesh):
    split = P("ctx", "tp")
    in_specs = (split,) * 5 + (P("tp", "ctx"), P(), P("ctx", None), P(None, "tp"), P(None, "tp"))
    return jax.shard_map(
        shards, mesh=mesh, in_specs=in_specs, out_specs=(split,) * 6, check_vma=False
    )
```

```python
import functools
import math

import jax
import jax.numpy as jnp
from jax import lax
from jax.experimental import pallas as pl
from jax.experimental.pallas import tpu as pltpu
from jax.sharding import PartitionSpec as P

BF = jnp.bfloat16
F32 = jnp.float32
MESH = pl.DeviceIdType.MESH
SCALE = 1.0 / math.sqrt(128)
LOG2E = math.log2(math.e)
NT = (((1,), (1,)), ((), ()))
TN = (((0,), (0,)), ((), ()))
SPAN = 128
TP = 8
NZ = 8
FEAT = 640
HALF_FEAT = 320
WROWS = 160

dot = functools.partial(lax.dot_general, preferred_element_type=F32)


def mm(a, b):
    return jnp.dot(a, b, preferred_element_type=F32)


def place():
    i = lax.axis_index("ctx")
    return i, i % 2, (i // 2) % NZ, i // 16


def ctx_of(y, z, core):
    return y * 16 + z * 2 + core


def remote(src, dst, send, recv, **where):
    return pltpu.make_async_remote_copy(
        src_ref=src, dst_ref=dst, send_sem=send, recv_sem=recv, device_id=where, device_id_type=MESH
    )


def kernel(
    swapped, q_hbm, k_hbm, v_hbm, o_hbm, d_hbm, ln_hbm, hid_hbm, wk, wv,
    dq_out, dk_out, dv_out, gk_out, gv_out, dh_out,
    q_in, k_in, v_in, o_in, d_in, ln_in, hid,
    qb, db, ob, lnc, lnb, deb, dqa, kv, acc, ysum_out, ysum_in, sum_out, sum_in, dqs, dqr,
    wbuf, dkv, gathered, part, cs, cr, gout, gin, fs, fr,
    lsem, xsend, xrecv, zsend, zrecv, ysend, yrecv, ysem_s, ysem_r, ssend, srecv,
    wsend, wrecv, fsend, frecv, dsem, tsend, trecv, csend, crecv, gsend, grecv,
):
    i, core, z, y = place()
    tp = lax.axis_index("tp")
    other = 1 - core
    chip = y * NZ + z
    odd = z % 2
    quad = z // 2
    ypart = ctx_of(1 - y, z, core)
    mate = ctx_of(y, z, other)

    def z_at(step):
        return (z + step + NZ) % NZ

    up_dev = ctx_of(y, z_at(1), core)
    down_dev = ctx_of(y, z_at(-1), core)
    reach = (3 + core, 4 - core)

    loads = [
        pltpu.make_async_copy(src, dst, lsem.at[n])
        for n, (src, dst) in enumerate(
            (
                (k_hbm, k_in), (v_hbm, v_in), (q_hbm, q_in), (d_hbm, d_in), (o_hbm, o_in),
                (ln_hbm, ln_in), (hid_hbm, hid),
                (wk.at[pl.ds(pl.multiple_of(tp * FEAT, FEAT), FEAT), :], wbuf.at[tp, 0]),
                (wv.at[pl.ds(pl.multiple_of(tp * FEAT, FEAT), FEAT), :], wbuf.at[tp, 1]),
            )
        )
    ]
    for load in loads:
        load.start()

    barrier = pltpu.get_barrier_semaphore()
    for dev in (ypart, mate):
        pl.semaphore_signal(barrier, inc=1, device_id={"ctx": dev}, device_id_type=MESH)
    for step in range(1, NZ):
        dev = ctx_of(y, z_at(step), core)
        pl.semaphore_signal(barrier, inc=1, device_id={"ctx": dev}, device_id_type=MESH)
        pl.semaphore_signal(
            barrier, inc=1, device_id={"tp": (tp + step) % TP}, device_id_type=MESH
        )

    flip_wide = jnp.concatenate([swapped[...]] * 16, axis=0)
    flip16 = flip_wide.astype(BF) > 0.5

    def canon(first, second, hl):
        return jnp.where(flip16, second, first) if hl == 0 else jnp.where(flip16, first, second)

    loads[0].wait()
    loads[1].wait()
    for hl in range(2):
        kv[y, z, 2 * hl] = canon(k_in[:SPAN, :], k_in[SPAN:, :], hl)
        kv[y, z, 2 * hl + 1] = canon(v_in[:SPAN, :], v_in[SPAN:, :], hl)
    pl.semaphore_wait(barrier, 2 * NZ)

    def hop(up, d):
        block = kv.at[y, z_at(-d if up else d)]
        return remote(
            block, block, zsend.at[up, d], zrecv.at[up, d + 1], ctx=up_dev if up else down_dev
        )

    def across(zz, act):
        @pl.when(y == 0)
        def _():
            block = kv.at[0, zz, 0:2]
            act(remote(block, block, ysend.at[zz], yrecv.at[zz], ctx=ypart))

        @pl.when(y == 1)
        def _():
            block = kv.at[1, zz]
            act(remote(block, block, ysend.at[zz], yrecv.at[zz], ctx=ypart))

    def across_wait(zz):
        @pl.when(y == 1)
        def _():
            block = kv.at[0, zz, 0:2]
            remote(block, block, ysend.at[zz], yrecv.at[zz], ctx=ypart).wait_recv()

        @pl.when(y == 0)
        def _():
            block = kv.at[1, zz]
            remote(block, block, ysend.at[zz], yrecv.at[zz], ctx=ypart).wait_recv()

    hop(1, 0).start()
    hop(0, 0).start()
    across(z, lambda copy: copy.start())

    for load in loads[2:6]:
        load.wait()
    for hl in range(2):
        for h in range(8):
            cols = slice(h * 128, (h + 1) * 128)
            for full, here in ((qb, q_in), (db, d_in), (ob, o_in)):
                full[core, hl, cols, :] = canon(here[:SPAN, cols], here[SPAN:, cols], hl)
    both = ln_in[...] * LOG2E
    flip8 = swapped[...] > 0.5
    lnc[core, 0] = jnp.where(flip8, both[:, SPAN:], both[:, :SPAN])
    lnc[core, 1] = jnp.where(flip8, both[:, :SPAN], both[:, SPAN:])
    swaps = [
        remote(ref.at[core], ref.at[core], xsend.at[n], xrecv.at[n], ctx=mate)
        for n, ref in enumerate((qb, db, ob, lnc))
    ]
    for swap in swaps:
        swap.start()

    def zero(n, _):
        for at in range(4):
            acc[n // NZ, n % NZ, at] = jnp.zeros((128, 128), F32)
        return 0

    lax.fori_loop(0, 2 * NZ, zero, 0)
    dqa[...] = jnp.zeros_like(dqa)

    ones = jnp.ones((128, 128), BF)
    head_of = lax.broadcasted_iota(jnp.int32, (32, 1024), 1) // 128
    pick = (lax.broadcasted_iota(jnp.int32, (32, 1024), 0) % 8 == head_of).astype(F32).astype(BF)

    def row_terms(slot):
        for hl in range(2):
            prod = db[slot, hl].astype(F32) * ob[slot, hl].astype(F32)
            high = prod.astype(BF)
            low = (prod - high.astype(F32)).astype(BF)
            deb[slot, hl] = mm(high, ones) + mm(low, ones)
            norm = lnc[slot, hl]
            p1 = norm.astype(BF)
            rest = norm - p1.astype(F32)
            p2 = rest.astype(BF)
            rest = rest - p2.astype(F32)
            p3 = rest.astype(BF)
            parts = jnp.concatenate(
                [p1.astype(F32), p2.astype(F32), p3.astype(F32), jnp.zeros((8, 128), F32)], axis=0
            ).astype(BF)
            wide = dot(parts, pick, TN)
            for h in range(8):
                lnb[slot, hl, h * 128 : (h + 1) * 128, :] = wide[:, h * 128 : (h + 1) * 128]

    row_terms(core)

    def pump(d):
        for up in (1, 0):

            @pl.when(d <= reach[up])
            def _():
                hop(up, d - 1).wait_recv()

                @pl.when(d < reach[up])
                def _():
                    hop(up, d).start()

                across(z_at(-d if up else d), lambda copy: copy.start())

    for swap in swaps:
        swap.wait()
    row_terms(other)
    pump(1)

    def unit(yp, w, hk, hq, masked):
        ra = 2 * w
        rb = 2 * w + 1
        k = jnp.concatenate([kv[yp, ra, 2 * hk], kv[yp, rb, 2 * hk]], axis=0)
        v = jnp.concatenate([kv[yp, ra, 2 * hk + 1], kv[yp, rb, 2 * hk + 1]], axis=0)
        gk = None
        gv = None
        for slot in range(2):
            q = qb[slot, hq]
            d = db[slot, hq]
            ln = lnb[slot, hq]
            de = deb[slot, hq]
            scores = dot(q, k, NT)
            dp = dot(d, v, NT)
            prob = jnp.exp2(scores * (SCALE * LOG2E) - jnp.concatenate([ln, ln], axis=1))
            if masked:
                qi = 2 * chip + slot
                qspan = jnp.where(hq == 0, qi, 63 - qi)
                shape = (1024, 128)
                gap = (
                    lax.broadcasted_iota(jnp.int32, shape, 0) % SPAN
                    - lax.broadcasted_iota(jnp.int32, shape, 1)
                )
                seen = []
                for rk in (ra, rb):
                    ki = 2 * (yp * NZ + rk) + core
                    kspan = jnp.where(hk == 0, ki, 63 - ki)
                    seen.append(gap >= (kspan - qspan) * SPAN)
                prob = jnp.concatenate(
                    [
                        jnp.where(seen[0], prob[:, :128], 0.0),
                        jnp.where(seen[1], prob[:, 128:], 0.0),
                    ],
                    axis=1,
                )
            ds = (prob * (dp - jnp.concatenate([de, de], axis=1))).astype(BF)
            pr = prob.astype(BF)
            dqa[slot, hq] += mm(ds, k)
            gk = dot(q, ds, TN) if gk is None else gk + dot(q, ds, TN)
            gv = dot(d, pr, TN) if gv is None else gv + dot(d, pr, TN)
        acc[yp, ra, 2 * hk] += gk[:, :128]
        acc[yp, rb, 2 * hk] += gk[:, 128:]
        acc[yp, ra, 2 * hk + 1] += gv[:, :128]
        acc[yp, rb, 2 * hk + 1] += gv[:, 128:]

    def pair_at(n):
        near = jnp.where(n == 1, 2 * odd - 1, 1 - 2 * odd)
        return (quad + jnp.where(n == 0, 0, jnp.where(n == 3, 2, near)) + 4) % 4

    def sum_across(zz, act):
        @pl.when(y == 0)
        def _():
            act(remote(ysum_out.at[zz], ysum_in.at[zz], ysem_s.at[zz], ysem_r.at[zz], ctx=ypart))

        @pl.when(y == 1)
        def _():
            src, dst = ysum_out.at[zz, 0:2], ysum_in.at[zz, 0:2]
            act(remote(src, dst, ysem_s.at[zz], ysem_r.at[zz], ctx=ypart))

    def sum_across_wait(zz):
        @pl.when(y == 1)
        def _():
            remote(
                ysum_out.at[zz], ysum_in.at[zz], ysem_s.at[zz], ysem_r.at[zz], ctx=ypart
            ).wait_recv()

        @pl.when(y == 0)
        def _():
            src, dst = ysum_out.at[zz, 0:2], ysum_in.at[zz, 0:2]
            remote(src, dst, ysem_s.at[zz], ysem_r.at[zz], ctx=ypart).wait_recv()

    def sum_home(zz):
        return remote(
            sum_out.at[zz], sum_in.at[z], ssend.at[zz], srecv.at[z], ctx=ctx_of(y, zz, core)
        )

    def send_across(n):
        w = pair_at(n)
        for zz in (2 * w, 2 * w + 1):
            ysum_out[zz] = acc[1 - y, zz].astype(BF)
            sum_across(zz, lambda copy: copy.start())

    def add_across(zz):
        sum_across_wait(zz)
        acc[y, zz, 0:2] += ysum_in[zz, 0:2].astype(F32)

        @pl.when(y == 1)
        def _():
            acc[y, zz, 2:4] += ysum_in[zz, 2:4].astype(F32)

    def send_home(n):
        w = pair_at(n)
        for zz in (2 * w, 2 * w + 1):
            add_across(zz)

            @pl.when(zz != z)
            def _():
                sum_out[zz] = acc[y, zz].astype(BF)
                sum_home(zz).start()

    def weight_copies(step):
        peer = (tp + step) % TP
        out = []
        for n, ref in enumerate((wk, wv)):
            rows = pl.ds(pl.multiple_of(peer * FEAT + core * HALF_FEAT, 64), HALF_FEAT)
            mine = pl.ds(pl.multiple_of(core * HALF_FEAT, 64), HALF_FEAT)
            out.append(
                remote(
                    ref.at[rows, :], wbuf.at[tp, n, mine, :],
                    wsend.at[step, n], wrecv.at[step, n], tp=peer,
                )
            )
        return out

    def weight_forwards(step):
        giver = (tp + TP - step) % TP
        out = []
        for n in range(2):
            mine = pl.ds(pl.multiple_of(core * HALF_FEAT, 64), HALF_FEAT)
            block = wbuf.at[giver, n, mine, :]
            out.append(remote(block, block, fsend.at[step, n], frecv.at[step, n], ctx=mate))
        return out

    def half_step(x, _):
        n = x // 2
        w = pair_at(n)
        far = jnp.where(x >= 6, 1 - x % 2, x % 2)
        yp = (y + far) % 2

        @pl.when(far == 1)
        def _():
            across_wait(2 * w)
            across_wait(2 * w + 1)

        @pl.when(x > 0)
        def _():
            for copy in weight_copies(x):
                copy.start()

        unit(yp, w, 0, 1, False)
        own = jnp.logical_and(far == 0, n == 0)

        @pl.when(own)
        def _():
            def masked_unit(hl, _):
                unit(yp, w, hl, hl, True)
                return 0

            lax.fori_loop(0, 2, masked_unit, 0)

        @pl.when(jnp.logical_not(own))
        def _():
            hl = jnp.where(yp * NZ + 2 * w < chip, 0, 1)
            unit(yp, w, hl, hl, False)

        @pl.when(far == 1)
        def _():
            send_across(n)

        for at, d in ((0, 2), (2, 3), (4, 4)):

            @pl.when(x == at)
            def _():
                pump(d)

        for at, done in ((3, 0), (5, 1), (6, 2), (7, 3)):

            @pl.when(x == at)
            def _():
                send_home(done)

        @pl.when(x > 1)
        def _():
            for copy in weight_copies(x - 1):
                copy.wait_recv()
            for copy in weight_forwards(x - 1):
                copy.start()

        return 0

    lax.fori_loop(0, 8, half_step, 0)

    dqs[...] = (dqa[other] * SCALE).astype(BF)
    dq_copy = remote(dqs, dqr, dsem.at[0], dsem.at[1], ctx=mate)
    dq_copy.start()
    for copy in weight_copies(TP - 1):
        copy.wait_recv()
    for copy in weight_forwards(TP - 1):
        copy.start()
    dq_copy.wait()
    for h in range(8):
        cols = slice(h * 128, (h + 1) * 128)
        low = (dqa[core, 0, cols, :] * SCALE + dqr[0, cols, :].astype(F32)).astype(BF)
        high = (dqa[core, 1, cols, :] * SCALE + dqr[1, cols, :].astype(F32)).astype(BF)
        dq_out[0:SPAN, cols] = jnp.where(flip16, high, low)
        dq_out[SPAN:, cols] = jnp.where(flip16, low, high)

    def collect(step, _):
        zz = z_at(step)
        remote(sum_out.at[zz], sum_in.at[zz], ssend.at[zz], srecv.at[zz], ctx=mate).wait_recv()
        for at in range(4):
            acc[y, z, at] += sum_in[zz, at].astype(F32)
        return 0

    lax.fori_loop(1, NZ, collect, 0)
    for out, at, factor in ((dk_out, 0, SCALE), (dv_out, 1, 1.0)):
        low = (acc[y, z, at] * factor).T.astype(BF)
        high = (acc[y, z, at + 2] * factor).T.astype(BF)
        cols = slice(at * 128, (at + 1) * 128)
        for rows, value in (
            (slice(0, SPAN), jnp.where(flip16, high, low)),
            (slice(SPAN, 2 * SPAN), jnp.where(flip16, low, high)),
        ):
            out[rows, :] = value
            dkv[rows, cols] = value

    def spread(step):
        return remote(dkv, gathered.at[tp], tsend.at[step], trecv.at[step], tp=(tp + step) % TP)

    for step in range(1, TP):
        spread(step).start()

    mine = dkv[...]
    loads[6].wait()

    def rows_of(yp, zz, k):
        return pl.ds(pl.multiple_of(((yp * NZ + zz) * 2 + k) * WROWS, 32), WROWS)

    def swap_part(yp):
        return remote(cs.at[yp], cr.at[yp], csend.at[yp], crecv.at[yp], ctx=mate)

    for yp in range(2):
        for n in range(5):
            at = yp * 2560 + n * 512
            part[at : at + 512, :] = dot(hid[:, at : at + 512], mine, TN)

        def fill(zz, _):
            cs[yp, zz] = part[rows_of(yp, zz, other), :].astype(BF)
            return 0

        lax.fori_loop(0, NZ, fill, 0)
        swap_part(yp).start()
    for yp in range(2):
        swap_part(yp).wait()

    def own_part(yp, zz):
        return part[rows_of(yp, zz, core), :] + cr[yp, zz].astype(F32)

    def arm(up, a, yp):
        return remote(
            gout.at[up, a, yp], gin.at[up, a - 1, yp],
            gsend.at[up, a, yp], grecv.at[up, a - 1, yp],
            ctx=up_dev if up else down_dev,
        )

    def arms(k, _):
        a = 4 - k
        for turn in range(2):
            yp = (1 - y) if turn == 0 else y
            for up in (1, 0):
                zz = (z + a) % NZ if up else (z - a + NZ) % NZ

                @pl.when(a == reach[up])
                def _():
                    gout[up, a, yp] = own_part(yp, zz).astype(BF)

                @pl.when(a < reach[up])
                def _():
                    arm(up, a + 1, yp).wait_recv()
                    gout[up, a, yp] = (own_part(yp, zz) + gin[up, a, yp].astype(F32)).astype(BF)

                @pl.when(a <= reach[up])
                def _():
                    arm(up, a, yp).start()

        return 0

    lax.fori_loop(0, 4, arms, 0)

    def plane_sum(yp):
        arm(1, 1, yp).wait_recv()
        arm(0, 1, yp).wait_recv()
        return own_part(yp, z) + gin[1, 0, yp].astype(F32) + gin[0, 0, yp].astype(F32)

    fs[...] = plane_sum(1 - y).astype(BF)
    f_copy = remote(fs, fr, dsem.at[2], dsem.at[3], ctx=ypart)
    f_copy.start()
    final = plane_sum(y)

    gathered[tp] = mine
    loads[7].wait()
    loads[8].wait()
    for step in range(1, TP):
        for copy in weight_forwards(step):
            copy.wait()
        spread(step).wait_recv()
    total = None
    for giver in range(TP):
        got = gathered[giver]
        term = dot(got[:, :128], wbuf[giver, 0], NT) + dot(got[:, 128:], wbuf[giver, 1], NT)
        total = term if total is None else total + term
    dh_out[...] = total.astype(BF)

    f_copy.wait()
    final = final + fr[...].astype(F32)
    gk_out[...] = final[:, :128]
    gv_out[...] = final[:, 128:]

    def drain(s, _):
        across(s, lambda copy: copy.wait_send())
        sum_across(s, lambda copy: copy.wait_send())

        @pl.when(s > 0)
        def _():
            for copy in weight_copies(s):
                copy.wait_send()
            sum_home(z_at(s)).wait_send()
            spread(s).wait_send()

        for up in (0, 1):

            @pl.when(s < reach[up])
            def _():
                hop(up, s).wait_send()
                for yp in range(2):
                    arm(up, s + 1, yp).wait_send()

        return 0

    lax.fori_loop(0, NZ, drain, 0)


def backward(*args):
    vmem = pl.BlockSpec(memory_space=pltpu.VMEM)
    hbm = pl.BlockSpec(memory_space=pl.ANY)
    dma = pltpu.SemaphoreType.DMA
    sds = jax.ShapeDtypeStruct
    rows = (2, 2, 1024, 128)
    block = (4, 128, 128)
    piece = (WROWS, 256)
    return pl.pallas_call(
        kernel,
        out_shape=[
            sds((256, 1024), BF),
            sds((256, 128), BF),
            sds((256, 128), BF),
            sds((WROWS, 128), F32),
            sds((WROWS, 128), F32),
            sds((256, FEAT), BF),
        ],
        in_specs=[vmem] + [hbm] * 9,
        out_specs=[vmem] * 6,
        scratch_shapes=[
            pltpu.VMEM((256, 1024), BF),
            pltpu.VMEM((256, 128), BF),
            pltpu.VMEM((256, 128), BF),
            pltpu.VMEM((256, 1024), BF),
            pltpu.VMEM((256, 1024), BF),
            pltpu.VMEM((8, 256), F32),
            pltpu.VMEM((256, 5120), BF),
            pltpu.VMEM(rows, BF),
            pltpu.VMEM(rows, BF),
            pltpu.VMEM(rows, BF),
            pltpu.VMEM((2, 2, 8, 128), F32),
            pltpu.VMEM(rows, F32),
            pltpu.VMEM(rows, F32),
            pltpu.VMEM(rows, F32),
            pltpu.VMEM((2, NZ) + block, BF),
            pltpu.VMEM((2, NZ) + block, F32),
            pltpu.VMEM((NZ,) + block, BF),
            pltpu.VMEM((NZ,) + block, BF),
            pltpu.VMEM((NZ,) + block, BF),
            pltpu.VMEM((NZ,) + block, BF),
            pltpu.VMEM((2, 1024, 128), BF),
            pltpu.VMEM((2, 1024, 128), BF),
            pltpu.VMEM((TP, 2, FEAT, 128), BF),
            pltpu.VMEM((256, 256), BF),
            pltpu.VMEM((TP, 256, 256), BF),
            pltpu.VMEM((5120, 256), F32),
            pltpu.VMEM((2, NZ) + piece, BF),
            pltpu.VMEM((2, NZ) + piece, BF),
            pltpu.VMEM((2, 5, 2) + piece, BF),
            pltpu.VMEM((2, 4, 2) + piece, BF),
            pltpu.VMEM(piece, BF),
            pltpu.VMEM(piece, BF),
            dma((9,)),
            dma((4,)),
            dma((4,)),
            dma((2, 5)),
            dma((2, 5)),
            dma((NZ,)),
            dma((NZ,)),
            dma((NZ,)),
            dma((NZ,)),
            dma((NZ,)),
            dma((NZ,)),
            dma((TP, 2)),
            dma((TP, 2)),
            dma((TP, 2)),
            dma((TP, 2)),
            dma((4,)),
            dma((TP,)),
            dma((TP,)),
            dma((2,)),
            dma((2,)),
            dma((2, 5, 2)),
            dma((2, 5, 2)),
        ],
        compiler_params=pltpu.CompilerParams(
            collective_id=0, has_side_effects=True, vmem_limit_bytes=58 * 2**20
        ),
        cost_estimate=pl.CostEstimate(
            flops=12 * 10**9, bytes_accessed=10**7, transcendentals=9 * 10**6
        ),
    )(*args)


def shards(q, k, v, o, d, ln, order, hidden, wk, wv):
    i = lax.axis_index("ctx")
    swapped = jnp.full((8, 128), (order[2 * i] != i).astype(F32))
    return tuple(backward(swapped, q, k, v, o, d, ln, hidden, wk, wv))


def solution(mesh):
    split = P("ctx", "tp")
    in_specs = (split,) * 5 + (P("tp", "ctx"), P(), P("ctx", None), P(None, "tp"), P(None, "tp"))
    return jax.shard_map(
        shards, mesh=mesh, in_specs=in_specs, out_specs=(split,) * 6, check_vma=False
    )
```

```python
import functools
import math

import jax
import jax.numpy as jnp
from jax import lax
from jax.experimental import pallas as pl
from jax.experimental.pallas import tpu as pltpu
from jax.sharding import PartitionSpec as P

BF = jnp.bfloat16
F32 = jnp.float32
MESH = pl.DeviceIdType.MESH
SCALE = 1.0 / math.sqrt(128)
LOG2E = math.log2(math.e)
NT = (((1,), (1,)), ((), ()))
TN = (((0,), (0,)), ((), ()))
SPAN = 128
TP = 8
NZ = 8
FEAT = 640
HALF_FEAT = 320
WROWS = 160

dot = functools.partial(lax.dot_general, preferred_element_type=F32)


def mm(a, b):
    return jnp.dot(a, b, preferred_element_type=F32)


def place():
    i = lax.axis_index("ctx")
    return i, i % 2, (i // 2) % NZ, i // 16


def ctx_of(y, z, core):
    return y * 16 + z * 2 + core


def remote(src, dst, send, recv, **where):
    return pltpu.make_async_remote_copy(
        src_ref=src, dst_ref=dst, send_sem=send, recv_sem=recv, device_id=where, device_id_type=MESH
    )


def kernel(
    order, q_hbm, k_hbm, v_hbm, o_hbm, d_hbm, ln_hbm, hid_hbm, wk, wv,
    dq_out, dk_out, dv_out, gk_out, gv_out, dh_out,
    q_in, k_in, v_in, o_in, d_in, ln_in, hid,
    qb, db, ob, lnc, lnb, deb, dqa, kv, acc, ysum_out, ysum_in, sum_out, sum_in, dqs, dqr,
    wbuf, dkv, gathered, part, cs, cr, gout, gin, fs, fr,
    lsem, xsend, xrecv, zsend, zrecv, ysend, yrecv, ysem_s, ysem_r, ssend, srecv,
    wsend, wrecv, fsend, frecv, dsem, tsend, trecv, csend, crecv, gsend, grecv,
):
    i, core, z, y = place()
    tp = lax.axis_index("tp")
    other = 1 - core
    chip = y * NZ + z
    odd = z % 2
    quad = z // 2
    ypart = ctx_of(1 - y, z, core)
    mate = ctx_of(y, z, other)

    def z_at(step):
        return (z + step + NZ) % NZ

    up_dev = ctx_of(y, z_at(1), core)
    down_dev = ctx_of(y, z_at(-1), core)
    reach = (3 + core, 4 - core)

    loads = [
        pltpu.make_async_copy(src, dst, lsem.at[n])
        for n, (src, dst) in enumerate(
            (
                (k_hbm, k_in), (v_hbm, v_in), (q_hbm, q_in), (d_hbm, d_in), (o_hbm, o_in),
                (ln_hbm, ln_in), (hid_hbm, hid),
                (wk.at[pl.ds(pl.multiple_of(tp * FEAT, FEAT), FEAT), :], wbuf.at[tp, 0]),
                (wv.at[pl.ds(pl.multiple_of(tp * FEAT, FEAT), FEAT), :], wbuf.at[tp, 1]),
            )
        )
    ]
    for load in loads:
        load.start()

    barrier = pltpu.get_barrier_semaphore()
    for dev in (ypart, mate):
        pl.semaphore_signal(barrier, inc=1, device_id={"ctx": dev}, device_id_type=MESH)
    for step in range(1, NZ):
        dev = ctx_of(y, z_at(step), core)
        pl.semaphore_signal(barrier, inc=1, device_id={"ctx": dev}, device_id_type=MESH)
        peer = (tp + step) % TP
        pl.semaphore_signal(barrier, inc=1, device_id={"tp": peer}, device_id_type=MESH)
        if step % 2:
            pl.semaphore_signal(
                barrier, inc=1, device_id={"ctx": ypart, "tp": peer}, device_id_type=MESH
            )

    flip8 = jnp.full((8, 128), order[2 * i], jnp.int32) != jnp.full((8, 128), i, jnp.int32)
    flip_wide = jnp.concatenate([jnp.where(flip8, 1.0, 0.0)] * 16, axis=0)
    flip16 = flip_wide.astype(BF) > 0.5

    def canon(first, second, hl):
        return jnp.where(flip16, second, first) if hl == 0 else jnp.where(flip16, first, second)

    loads[0].wait()
    loads[1].wait()
    for hl in range(2):
        kv[y, z, 2 * hl] = canon(k_in[:SPAN, :], k_in[SPAN:, :], hl)
        kv[y, z, 2 * hl + 1] = canon(v_in[:SPAN, :], v_in[SPAN:, :], hl)
    pl.semaphore_wait(barrier, 2 * NZ + TP // 2)

    def hop(up, d):
        block = kv.at[y, z_at(-d if up else d)]
        return remote(
            block, block, zsend.at[up, d], zrecv.at[up, d + 1], ctx=up_dev if up else down_dev
        )

    def across(zz, act):
        @pl.when(y == 0)
        def _():
            block = kv.at[0, zz, 0:2]
            act(remote(block, block, ysend.at[zz], yrecv.at[zz], ctx=ypart))

        @pl.when(y == 1)
        def _():
            block = kv.at[1, zz]
            act(remote(block, block, ysend.at[zz], yrecv.at[zz], ctx=ypart))

    def across_wait(zz):
        @pl.when(y == 1)
        def _():
            block = kv.at[0, zz, 0:2]
            remote(block, block, ysend.at[zz], yrecv.at[zz], ctx=ypart).wait_recv()

        @pl.when(y == 0)
        def _():
            block = kv.at[1, zz]
            remote(block, block, ysend.at[zz], yrecv.at[zz], ctx=ypart).wait_recv()

    hop(1, 0).start()
    hop(0, 0).start()
    across(z, lambda copy: copy.start())

    for load in loads[2:6]:
        load.wait()
    for hl in range(2):
        for h in range(8):
            cols = slice(h * 128, (h + 1) * 128)
            for full, here in ((qb, q_in), (db, d_in), (ob, o_in)):
                full[core, hl, cols, :] = canon(here[:SPAN, cols], here[SPAN:, cols], hl)
    both = ln_in[...] * LOG2E
    lnc[core, 0] = jnp.where(flip8, both[:, SPAN:], both[:, :SPAN])
    lnc[core, 1] = jnp.where(flip8, both[:, :SPAN], both[:, SPAN:])
    swaps = [
        remote(ref.at[core], ref.at[core], xsend.at[n], xrecv.at[n], ctx=mate)
        for n, ref in enumerate((qb, db, ob, lnc))
    ]
    for swap in swaps:
        swap.start()

    def zero(n, _):
        for at in range(4):
            acc[n // NZ, n % NZ, at] = jnp.zeros((128, 128), F32)
        return 0

    lax.fori_loop(0, 2 * NZ, zero, 0)
    dqa[...] = jnp.zeros_like(dqa)

    ones = jnp.ones((128, 128), BF)
    head_of = lax.broadcasted_iota(jnp.int32, (32, 1024), 1) // 128
    pick = (lax.broadcasted_iota(jnp.int32, (32, 1024), 0) % 8 == head_of).astype(F32).astype(BF)

    def row_terms(slot):
        for hl in range(2):
            prod = db[slot, hl].astype(F32) * ob[slot, hl].astype(F32)
            high = prod.astype(BF)
            low = (prod - high.astype(F32)).astype(BF)
            deb[slot, hl] = mm(high, ones) + mm(low, ones)
            norm = lnc[slot, hl]
            p1 = norm.astype(BF)
            rest = norm - p1.astype(F32)
            p2 = rest.astype(BF)
            rest = rest - p2.astype(F32)
            p3 = rest.astype(BF)
            parts = jnp.concatenate(
                [p1.astype(F32), p2.astype(F32), p3.astype(F32), jnp.zeros((8, 128), F32)], axis=0
            ).astype(BF)
            wide = dot(parts, pick, TN)
            for h in range(8):
                lnb[slot, hl, h * 128 : (h + 1) * 128, :] = wide[:, h * 128 : (h + 1) * 128]

    row_terms(core)

    def pump(d):
        for up in (1, 0):

            @pl.when(d <= reach[up])
            def _():
                hop(up, d - 1).wait_recv()

                @pl.when(d < reach[up])
                def _():
                    hop(up, d).start()

                across(z_at(-d if up else d), lambda copy: copy.start())

    pump(1)
    for swap in swaps:
        swap.wait()
    row_terms(other)
    pump(2)

    def unit(yp, w, hk, hq, masked):
        ra = 2 * w
        rb = 2 * w + 1
        k = jnp.concatenate([kv[yp, ra, 2 * hk], kv[yp, rb, 2 * hk]], axis=0)
        v = jnp.concatenate([kv[yp, ra, 2 * hk + 1], kv[yp, rb, 2 * hk + 1]], axis=0)
        gk = None
        gv = None
        for slot in range(2):
            q = qb[slot, hq]
            d = db[slot, hq]
            ln = lnb[slot, hq]
            de = deb[slot, hq]
            scores = dot(q, k, NT)
            dp = dot(d, v, NT)
            prob = jnp.exp2(scores * (SCALE * LOG2E) - jnp.concatenate([ln, ln], axis=1))
            if masked:
                qi = 2 * chip + slot
                qspan = jnp.where(hq == 0, qi, 63 - qi)
                shape = (1024, 128)
                gap = (
                    lax.broadcasted_iota(jnp.int32, shape, 0) % SPAN
                    - lax.broadcasted_iota(jnp.int32, shape, 1)
                )
                seen = []
                for rk in (ra, rb):
                    ki = 2 * (yp * NZ + rk) + core
                    kspan = jnp.where(hk == 0, ki, 63 - ki)
                    seen.append(gap >= (kspan - qspan) * SPAN)
                prob = jnp.concatenate(
                    [
                        jnp.where(seen[0], prob[:, :128], 0.0),
                        jnp.where(seen[1], prob[:, 128:], 0.0),
                    ],
                    axis=1,
                )
            ds = (prob * (dp - jnp.concatenate([de, de], axis=1))).astype(BF)
            pr = prob.astype(BF)
            dqa[slot, hq] += mm(ds, k)
            gk = dot(q, ds, TN) if gk is None else gk + dot(q, ds, TN)
            gv = dot(d, pr, TN) if gv is None else gv + dot(d, pr, TN)
        acc[yp, ra, 2 * hk] += gk[:, :128]
        acc[yp, rb, 2 * hk] += gk[:, 128:]
        acc[yp, ra, 2 * hk + 1] += gv[:, :128]
        acc[yp, rb, 2 * hk + 1] += gv[:, 128:]

    def pair_at(n):
        near = jnp.where(n == 2, 1 - 2 * odd, 2 * odd - 1)
        return (quad + jnp.where(n == 0, 0, jnp.where(n == 1, 2, near)) + 4) % 4

    def sum_across(zz, act):
        @pl.when(y == 0)
        def _():
            act(remote(ysum_out.at[zz], ysum_in.at[zz], ysem_s.at[zz], ysem_r.at[zz], ctx=ypart))

        @pl.when(y == 1)
        def _():
            src, dst = ysum_out.at[zz, 0:2], ysum_in.at[zz, 0:2]
            act(remote(src, dst, ysem_s.at[zz], ysem_r.at[zz], ctx=ypart))

    def sum_across_wait(zz):
        @pl.when(y == 1)
        def _():
            remote(
                ysum_out.at[zz], ysum_in.at[zz], ysem_s.at[zz], ysem_r.at[zz], ctx=ypart
            ).wait_recv()

        @pl.when(y == 0)
        def _():
            src, dst = ysum_out.at[zz, 0:2], ysum_in.at[zz, 0:2]
            remote(src, dst, ysem_s.at[zz], ysem_r.at[zz], ctx=ypart).wait_recv()

    def sum_home(zz):
        return remote(
            sum_out.at[zz], sum_in.at[z], ssend.at[zz], srecv.at[z], ctx=ctx_of(y, zz, core)
        )

    def send_across(n):
        w = pair_at(n)
        for zz in (2 * w, 2 * w + 1):
            ysum_out[zz] = acc[1 - y, zz].astype(BF)
            sum_across(zz, lambda copy: copy.start())

    def add_across(zz):
        sum_across_wait(zz)
        acc[y, zz, 0:2] += ysum_in[zz, 0:2].astype(F32)

        @pl.when(y == 1)
        def _():
            acc[y, zz, 2:4] += ysum_in[zz, 2:4].astype(F32)

    def send_home(n):
        w = pair_at(n)
        for zz in (2 * w, 2 * w + 1):
            add_across(zz)

            @pl.when(zz != z)
            def _():
                sum_out[zz] = acc[y, zz].astype(BF)
                sum_home(zz).start()

    def weight_copies(step):
        peer = (tp + step) % TP
        out = []
        for n, ref in enumerate((wk, wv)):
            rows = pl.ds(pl.multiple_of(peer * FEAT + core * HALF_FEAT, 64), HALF_FEAT)
            mine = pl.ds(pl.multiple_of(core * HALF_FEAT, 64), HALF_FEAT)
            out.append(
                remote(
                    ref.at[rows, :], wbuf.at[tp, n, mine, :],
                    wsend.at[step, n], wrecv.at[step, n], tp=peer, ctx=jnp.where(step % 2 == 1, ypart, i),
                )
            )
        return out

    def weight_forwards(step):
        giver = (tp + TP - step) % TP
        out = []
        for n in range(2):
            mine = pl.ds(pl.multiple_of(core * HALF_FEAT, 64), HALF_FEAT)
            block = wbuf.at[giver, n, mine, :]
            out.append(remote(block, block, fsend.at[step, n], frecv.at[step, n], ctx=mate))
        return out

    def half_step(x, _):
        n = jnp.where(x < 4, x // 2, 2 + x % 2)
        w = pair_at(n)
        far = jnp.where(x < 4, x % 2, jnp.where(x < 6, 1, 0))
        yp = (y + far) % 2

        @pl.when(far == 1)
        def _():
            across_wait(2 * w)
            across_wait(2 * w + 1)

        @pl.when(x < 7)
        def _():
            for copy in weight_copies(x + 1):
                copy.start()

        unit(yp, w, 0, 1, False)
        own = jnp.logical_and(far == 0, n == 0)

        @pl.when(own)
        def _():
            def masked_unit(hl, _):
                unit(yp, w, hl, hl, True)
                return 0

            lax.fori_loop(0, 2, masked_unit, 0)

        @pl.when(jnp.logical_not(own))
        def _():
            hl = jnp.where(yp * NZ + 2 * w < chip, 0, 1)
            unit(yp, w, hl, hl, False)

        @pl.when(far == 1)
        def _():
            send_across(n)

        for at, d in ((0, 3), (1, 4)):

            @pl.when(x == at)
            def _():
                pump(d)

        for at, done in ((3, 0), (5, 1), (6, 2), (7, 3)):

            @pl.when(x == at)
            def _():
                send_home(done)

        @pl.when(x > 1)
        def _():
            for copy in weight_copies(x - 1):
                copy.wait_recv()
            for copy in weight_forwards(x - 1):
                copy.start()

        return 0

    lax.fori_loop(0, 8, half_step, 0)

    dqs[...] = (dqa[other] * SCALE).astype(BF)
    dq_copy = remote(dqs, dqr, dsem.at[0], dsem.at[1], ctx=mate)
    dq_copy.start()
    for copy in weight_copies(TP - 1):
        copy.wait_recv()
    for copy in weight_forwards(TP - 1):
        copy.start()
    dq_copy.wait()
    for h in range(8):
        cols = slice(h * 128, (h + 1) * 128)
        low = (dqa[core, 0, cols, :] * SCALE + dqr[0, cols, :].astype(F32)).astype(BF)
        high = (dqa[core, 1, cols, :] * SCALE + dqr[1, cols, :].astype(F32)).astype(BF)
        dq_out[0:SPAN, cols] = jnp.where(flip16, high, low)
        dq_out[SPAN:, cols] = jnp.where(flip16, low, high)

    def collect(step, _):
        zz = z_at(step)
        remote(sum_out.at[zz], sum_in.at[zz], ssend.at[zz], srecv.at[zz], ctx=mate).wait_recv()
        for at in range(4):
            acc[y, z, at] += sum_in[zz, at].astype(F32)
        return 0

    lax.fori_loop(1, NZ, collect, 0)
    for out, at, factor in ((dk_out, 0, SCALE), (dv_out, 1, 1.0)):
        low = (acc[y, z, at] * factor).T.astype(BF)
        high = (acc[y, z, at + 2] * factor).T.astype(BF)
        cols = slice(at * 128, (at + 1) * 128)
        for rows, value in (
            (slice(0, SPAN), jnp.where(flip16, high, low)),
            (slice(SPAN, 2 * SPAN), jnp.where(flip16, low, high)),
        ):
            out[rows, :] = value
            dkv[rows, cols] = value

    def spread(step):
        return remote(dkv, gathered.at[tp], tsend.at[step], trecv.at[step], tp=(tp + step) % TP)

    for step in range(1, TP):
        spread(step).start()

    mine = dkv[...]
    loads[6].wait()

    def rows_of(yp, zz, k):
        return pl.ds(pl.multiple_of(((yp * NZ + zz) * 2 + k) * WROWS, 32), WROWS)

    def swap_part(yp):
        return remote(cs.at[yp], cr.at[yp], csend.at[yp], crecv.at[yp], ctx=mate)

    for turn in range(2):
        yp = (1 - y) if turn == 0 else y
        for n in range(5):
            at = pl.ds(pl.multiple_of(yp * 2560 + n * 512, 512), 512)
            part[at, :] = dot(hid[:, at], mine, TN)

        def fill(zz, _):
            cs[yp, zz] = part[rows_of(yp, zz, other), :].astype(BF)
            return 0

        lax.fori_loop(0, NZ, fill, 0)
        swap_part(yp).start()
    def own_part(yp, zz):
        return part[rows_of(yp, zz, core), :] + cr[yp, zz].astype(F32)

    def arm(up, a, yp):
        return remote(
            gout.at[up, a, yp], gin.at[up, a - 1, yp],
            gsend.at[up, a, yp], grecv.at[up, a - 1, yp],
            ctx=up_dev if up else down_dev,
        )

    def arms(k, _):
        a = 4 - k
        for turn in range(2):
            yp = (1 - y) if turn == 0 else y

            @pl.when(k == 0)
            def _():
                swap_part(yp).wait()

            for up in (1, 0):
                zz = (z + a) % NZ if up else (z - a + NZ) % NZ

                @pl.when(a == reach[up])
                def _():
                    gout[up, a, yp] = own_part(yp, zz).astype(BF)

                @pl.when(a < reach[up])
                def _():
                    arm(up, a + 1, yp).wait_recv()
                    gout[up, a, yp] = (own_part(yp, zz) + gin[up, a, yp].astype(F32)).astype(BF)

                @pl.when(a <= reach[up])
                def _():
                    arm(up, a, yp).start()

        return 0

    lax.fori_loop(0, 4, arms, 0)

    def plane_sum(yp):
        arm(1, 1, yp).wait_recv()
        arm(0, 1, yp).wait_recv()
        return own_part(yp, z) + gin[1, 0, yp].astype(F32) + gin[0, 0, yp].astype(F32)

    fs[...] = plane_sum(1 - y).astype(BF)
    f_copy = remote(fs, fr, dsem.at[2], dsem.at[3], ctx=ypart)
    f_copy.start()
    final = plane_sum(y)

    gathered[tp] = mine
    loads[7].wait()
    loads[8].wait()
    for step in range(1, TP):
        for copy in weight_forwards(step):
            copy.wait()
        spread(step).wait_recv()
    total = None
    for giver in range(TP):
        got = gathered[giver]
        term = dot(got[:, :128], wbuf[giver, 0], NT) + dot(got[:, 128:], wbuf[giver, 1], NT)
        total = term if total is None else total + term
    dh_out[...] = total.astype(BF)

    f_copy.wait()
    final = final + fr[...].astype(F32)
    gk_out[...] = final[:, :128]
    gv_out[...] = final[:, 128:]

    def drain(s, _):
        across(s, lambda copy: copy.wait_send())
        sum_across(s, lambda copy: copy.wait_send())

        @pl.when(s > 0)
        def _():
            for copy in weight_copies(s):
                copy.wait_send()
            sum_home(z_at(s)).wait_send()
            spread(s).wait_send()

        for up in (0, 1):

            @pl.when(s < reach[up])
            def _():
                hop(up, s).wait_send()
                for yp in range(2):
                    arm(up, s + 1, yp).wait_send()

        return 0

    lax.fori_loop(0, NZ, drain, 0)


def backward(*args):
    vmem = pl.BlockSpec(memory_space=pltpu.VMEM)
    hbm = pl.BlockSpec(memory_space=pl.ANY)
    dma = pltpu.SemaphoreType.DMA
    sds = jax.ShapeDtypeStruct
    rows = (2, 2, 1024, 128)
    block = (4, 128, 128)
    piece = (WROWS, 256)
    return pl.pallas_call(
        kernel,
        out_shape=[
            sds((256, 1024), BF),
            sds((256, 128), BF),
            sds((256, 128), BF),
            sds((WROWS, 128), F32),
            sds((WROWS, 128), F32),
            sds((256, FEAT), BF),
        ],
        in_specs=[pl.BlockSpec(memory_space=pltpu.SMEM)] + [hbm] * 9,
        out_specs=[vmem] * 6,
        scratch_shapes=[
            pltpu.VMEM((256, 1024), BF),
            pltpu.VMEM((256, 128), BF),
            pltpu.VMEM((256, 128), BF),
            pltpu.VMEM((256, 1024), BF),
            pltpu.VMEM((256, 1024), BF),
            pltpu.VMEM((8, 256), F32),
            pltpu.VMEM((256, 5120), BF),
            pltpu.VMEM(rows, BF),
            pltpu.VMEM(rows, BF),
            pltpu.VMEM(rows, BF),
            pltpu.VMEM((2, 2, 8, 128), F32),
            pltpu.VMEM(rows, F32),
            pltpu.VMEM(rows, F32),
            pltpu.VMEM(rows, F32),
            pltpu.VMEM((2, NZ) + block, BF),
            pltpu.VMEM((2, NZ) + block, F32),
            pltpu.VMEM((NZ,) + block, BF),
            pltpu.VMEM((NZ,) + block, BF),
            pltpu.VMEM((NZ,) + block, BF),
            pltpu.VMEM((NZ,) + block, BF),
            pltpu.VMEM((2, 1024, 128), BF),
            pltpu.VMEM((2, 1024, 128), BF),
            pltpu.VMEM((TP, 2, FEAT, 128), BF),
            pltpu.VMEM((256, 256), BF),
            pltpu.VMEM((TP, 256, 256), BF),
            pltpu.VMEM((5120, 256), F32),
            pltpu.VMEM((2, NZ) + piece, BF),
            pltpu.VMEM((2, NZ) + piece, BF),
            pltpu.VMEM((2, 5, 2) + piece, BF),
            pltpu.VMEM((2, 4, 2) + piece, BF),
            pltpu.VMEM(piece, BF),
            pltpu.VMEM(piece, BF),
            dma((9,)),
            dma((4,)),
            dma((4,)),
            dma((2, 5)),
            dma((2, 5)),
            dma((NZ,)),
            dma((NZ,)),
            dma((NZ,)),
            dma((NZ,)),
            dma((NZ,)),
            dma((NZ,)),
            dma((TP, 2)),
            dma((TP, 2)),
            dma((TP, 2)),
            dma((TP, 2)),
            dma((4,)),
            dma((TP,)),
            dma((TP,)),
            dma((2,)),
            dma((2,)),
            dma((2, 5, 2)),
            dma((2, 5, 2)),
        ],
        compiler_params=pltpu.CompilerParams(
            collective_id=0, has_side_effects=True, vmem_limit_bytes=58 * 2**20
        ),
        cost_estimate=pl.CostEstimate(
            flops=12 * 10**9, bytes_accessed=10**7, transcendentals=9 * 10**6
        ),
    )(*args)


def copy_kernel(*refs):
    sems = refs[18]
    inward = [pltpu.make_async_copy(refs[n], refs[12 + n], sems.at[0, n]) for n in range(6)]
    outward = [pltpu.make_async_copy(refs[12 + n], refs[6 + n], sems.at[1, n]) for n in range(6)]
    for copy in inward:
        copy.start()
    for n in range(6):
        inward[n].wait()
        outward[n].start()
    for copy in outward:
        copy.wait()


def place_outputs(*outs):
    hbm = pl.BlockSpec(memory_space=pl.ANY)
    return pl.pallas_call(
        copy_kernel,
        out_shape=[jax.ShapeDtypeStruct(a.shape, a.dtype) for a in outs],
        in_specs=[hbm] * 6,
        out_specs=[hbm] * 6,
        scratch_shapes=[pltpu.VMEM(a.shape, a.dtype) for a in outs]
        + [pltpu.SemaphoreType.DMA((2, 6))],
        compiler_params=pltpu.CompilerParams(vmem_limit_bytes=60 * 2**20),
    )(*outs)


def shards(q, k, v, o, d, ln, order, hidden, wk, wv):
    return tuple(place_outputs(*backward(order, q, k, v, o, d, ln, hidden, wk, wv)))


def solution(mesh):
    split = P("ctx", "tp")
    in_specs = (split,) * 5 + (P("tp", "ctx"), P(), P("ctx", None), P(None, "tp"), P(None, "tp"))
    return jax.shard_map(
        shards, mesh=mesh, in_specs=in_specs, out_specs=(split,) * 6, check_vma=False
    )
```

```python
import functools
import math

import jax
import jax.numpy as jnp
from jax import lax
from jax.experimental import pallas as pl
from jax.experimental.pallas import tpu as pltpu
from jax.sharding import PartitionSpec as P

BF = jnp.bfloat16
F32 = jnp.float32
MESH = pl.DeviceIdType.MESH
SCALE = 1.0 / math.sqrt(128)
LOG2E = math.log2(math.e)
NT = (((1,), (1,)), ((), ()))
TN = (((0,), (0,)), ((), ()))
SPAN = 128
TP = 8
NZ = 8
FEAT = 640
HALF_FEAT = 320
WROWS = 160

dot = functools.partial(lax.dot_general, preferred_element_type=F32)


def mm(a, b):
    return jnp.dot(a, b, preferred_element_type=F32)


def place():
    i = lax.axis_index("ctx")
    return i, i % 2, (i // 2) % NZ, i // 16


def ctx_of(y, z, core):
    return y * 16 + z * 2 + core


def remote(src, dst, send, recv, **where):
    return pltpu.make_async_remote_copy(
        src_ref=src, dst_ref=dst, send_sem=send, recv_sem=recv, device_id=where, device_id_type=MESH
    )


def kernel(
    order, q_hbm, k_hbm, v_hbm, o_hbm, d_hbm, ln_hbm, hid_hbm, wk, wv,
    dq_out, dk_out, dv_out, gk_out, gv_out, dh_out,
    q_in, k_in, v_in, o_in, d_in, ln_in, hid,
    qb, db, ob, lnc, lnb, deb, dqa, kv, acc, ysum_out, ysum_in, sum_out, sum_in, home_in, dqs, dqr,
    wbuf, dkv, gathered, part, cs, cr, gout, gin, fs, fr,
    lsem, xsend, xrecv, zsend, zrecv, ysend, yrecv, ysem_s, ysem_r, ssend, srecv, homer,
    wsend, wrecv, fsend, frecv, dsem, tsend, trecv, csend, crecv, gsend, grecv,
):
    i, core, z, y = place()
    tp = lax.axis_index("tp")
    other = 1 - core
    chip = y * NZ + z
    odd = z % 2
    quad = z // 2
    ypart = ctx_of(1 - y, z, core)
    mate = ctx_of(y, z, other)

    def z_at(step):
        return (z + step + NZ) % NZ

    up_dev = ctx_of(y, z_at(1), core)
    down_dev = ctx_of(y, z_at(-1), core)
    reach = (3 + core, 4 - core)

    loads = [
        pltpu.make_async_copy(src, dst, lsem.at[n])
        for n, (src, dst) in enumerate(
            (
                (k_hbm, k_in), (v_hbm, v_in), (q_hbm, q_in), (d_hbm, d_in), (o_hbm, o_in),
                (ln_hbm, ln_in), (hid_hbm, hid),
                (wk.at[pl.ds(pl.multiple_of(tp * FEAT, FEAT), FEAT), :], wbuf.at[tp, 0]),
                (wv.at[pl.ds(pl.multiple_of(tp * FEAT, FEAT), FEAT), :], wbuf.at[tp, 1]),
            )
        )
    ]
    for load in loads:
        load.start()

    barrier = pltpu.get_barrier_semaphore()
    for dev in (ypart, mate):
        pl.semaphore_signal(barrier, inc=1, device_id={"ctx": dev}, device_id_type=MESH)
    for step in range(1, NZ):
        dev = ctx_of(y, z_at(step), core)
        pl.semaphore_signal(barrier, inc=1, device_id={"ctx": dev}, device_id_type=MESH)
        peer = (tp + step) % TP
        pl.semaphore_signal(barrier, inc=1, device_id={"tp": peer}, device_id_type=MESH)
        if step % 2:
            pl.semaphore_signal(
                barrier, inc=1, device_id={"ctx": ypart, "tp": peer}, device_id_type=MESH
            )

    flip8 = jnp.full((8, 128), order[2 * i], jnp.int32) != jnp.full((8, 128), i, jnp.int32)
    flip_wide = jnp.concatenate([jnp.where(flip8, 1.0, 0.0)] * 16, axis=0)
    flip16 = flip_wide.astype(BF) > 0.5

    def canon(first, second, hl):
        return jnp.where(flip16, second, first) if hl == 0 else jnp.where(flip16, first, second)

    loads[0].wait()
    loads[1].wait()
    for hl in range(2):
        kv[y, z, 2 * hl] = canon(k_in[:SPAN, :], k_in[SPAN:, :], hl)
        kv[y, z, 2 * hl + 1] = canon(v_in[:SPAN, :], v_in[SPAN:, :], hl)
    pl.semaphore_wait(barrier, 2 * NZ + TP // 2)

    def hop(up, d):
        block = kv.at[y, z_at(-d if up else d)]
        return remote(
            block, block, zsend.at[up, d], zrecv.at[up, d + 1], ctx=up_dev if up else down_dev
        )

    def across(zz, act):
        @pl.when(y == 0)
        def _():
            block = kv.at[0, zz, 0:2]
            act(remote(block, block, ysend.at[zz], yrecv.at[zz], ctx=ypart))

        @pl.when(y == 1)
        def _():
            block = kv.at[1, zz]
            act(remote(block, block, ysend.at[zz], yrecv.at[zz], ctx=ypart))

    def across_wait(zz):
        @pl.when(y == 1)
        def _():
            block = kv.at[0, zz, 0:2]
            remote(block, block, ysend.at[zz], yrecv.at[zz], ctx=ypart).wait_recv()

        @pl.when(y == 0)
        def _():
            block = kv.at[1, zz]
            remote(block, block, ysend.at[zz], yrecv.at[zz], ctx=ypart).wait_recv()

    hop(1, 0).start()
    hop(0, 0).start()
    across(z, lambda copy: copy.start())

    for load in loads[2:6]:
        load.wait()
    for hl in range(2):
        for h in range(8):
            cols = slice(h * 128, (h + 1) * 128)
            for full, here in ((qb, q_in), (db, d_in), (ob, o_in)):
                full[core, hl, cols, :] = canon(here[:SPAN, cols], here[SPAN:, cols], hl)
    both = ln_in[...] * LOG2E
    lnc[core, 0] = jnp.where(flip8, both[:, SPAN:], both[:, :SPAN])
    lnc[core, 1] = jnp.where(flip8, both[:, :SPAN], both[:, SPAN:])
    swaps = [
        remote(ref.at[core], ref.at[core], xsend.at[n], xrecv.at[n], ctx=mate)
        for n, ref in enumerate((qb, db, ob, lnc))
    ]
    for swap in swaps:
        swap.start()

    def zero(n, _):
        for at in range(4):
            acc[n // NZ, n % NZ, at] = jnp.zeros((128, 128), F32)
        return 0

    lax.fori_loop(0, 2 * NZ, zero, 0)
    dqa[...] = jnp.zeros_like(dqa)

    ones = jnp.ones((128, 128), BF)
    head_of = lax.broadcasted_iota(jnp.int32, (32, 1024), 1) // 128
    pick = (lax.broadcasted_iota(jnp.int32, (32, 1024), 0) % 8 == head_of).astype(F32).astype(BF)

    def row_terms(slot):
        for hl in range(2):
            prod = db[slot, hl].astype(F32) * ob[slot, hl].astype(F32)
            high = prod.astype(BF)
            low = (prod - high.astype(F32)).astype(BF)
            deb[slot, hl] = mm(high, ones) + mm(low, ones)
            norm = lnc[slot, hl]
            p1 = norm.astype(BF)
            rest = norm - p1.astype(F32)
            p2 = rest.astype(BF)
            rest = rest - p2.astype(F32)
            p3 = rest.astype(BF)
            parts = jnp.concatenate(
                [p1.astype(F32), p2.astype(F32), p3.astype(F32), jnp.zeros((8, 128), F32)], axis=0
            ).astype(BF)
            wide = dot(parts, pick, TN)
            for h in range(8):
                lnb[slot, hl, h * 128 : (h + 1) * 128, :] = wide[:, h * 128 : (h + 1) * 128]

    row_terms(core)

    def pump(d):
        for up in (1, 0):

            @pl.when(d <= reach[up])
            def _():
                hop(up, d - 1).wait_recv()

                @pl.when(d < reach[up])
                def _():
                    hop(up, d).start()

                across(z_at(-d if up else d), lambda copy: copy.start())

    pump(1)
    for swap in swaps:
        swap.wait()
    row_terms(other)

    def unit(yp, w, hk, hq, masked):
        ra = 2 * w
        rb = 2 * w + 1
        k = jnp.concatenate([kv[yp, ra, 2 * hk], kv[yp, rb, 2 * hk]], axis=0)
        v = jnp.concatenate([kv[yp, ra, 2 * hk + 1], kv[yp, rb, 2 * hk + 1]], axis=0)
        gk = None
        gv = None
        for slot in range(2):
            q = qb[slot, hq]
            d = db[slot, hq]
            ln = lnb[slot, hq]
            de = deb[slot, hq]
            scores = dot(q, k, NT)
            dp = dot(d, v, NT)
            prob = jnp.exp2(scores * (SCALE * LOG2E) - jnp.concatenate([ln, ln], axis=1))
            if masked:
                qi = 2 * chip + slot
                qspan = jnp.where(hq == 0, qi, 63 - qi)
                shape = (1024, 128)
                gap = (
                    lax.broadcasted_iota(jnp.int32, shape, 0) % SPAN
                    - lax.broadcasted_iota(jnp.int32, shape, 1)
                )
                seen = []
                for rk in (ra, rb):
                    ki = 2 * (yp * NZ + rk) + core
                    kspan = jnp.where(hk == 0, ki, 63 - ki)
                    seen.append(gap >= (kspan - qspan) * SPAN)
                prob = jnp.concatenate(
                    [
                        jnp.where(seen[0], prob[:, :128], 0.0),
                        jnp.where(seen[1], prob[:, 128:], 0.0),
                    ],
                    axis=1,
                )
            ds = (prob * (dp - jnp.concatenate([de, de], axis=1))).astype(BF)
            pr = prob.astype(BF)
            dqa[slot, hq] += mm(ds, k)
            gk = dot(q, ds, TN) if gk is None else gk + dot(q, ds, TN)
            gv = dot(d, pr, TN) if gv is None else gv + dot(d, pr, TN)
        acc[yp, ra, 2 * hk] += gk[:, :128]
        acc[yp, rb, 2 * hk] += gk[:, 128:]
        acc[yp, ra, 2 * hk + 1] += gv[:, :128]
        acc[yp, rb, 2 * hk + 1] += gv[:, 128:]

    def pair_at(n):
        side = jnp.where(n == 1, 2 * odd - 1, 1 - 2 * odd)
        return (quad + jnp.where(n == 0, 0, jnp.where(n == 2, 2, side)) + 4) % 4

    def sum_across(zz, act):
        @pl.when(y == 0)
        def _():
            act(remote(ysum_out.at[zz], ysum_in.at[zz], ysem_s.at[zz], ysem_r.at[zz], ctx=ypart))

        @pl.when(y == 1)
        def _():
            src, dst = ysum_out.at[zz, 0:2], ysum_in.at[zz, 0:2]
            act(remote(src, dst, ysem_s.at[zz], ysem_r.at[zz], ctx=ypart))

    def sum_across_wait(zz):
        @pl.when(y == 1)
        def _():
            remote(
                ysum_out.at[zz], ysum_in.at[zz], ysem_s.at[zz], ysem_r.at[zz], ctx=ypart
            ).wait_recv()

        @pl.when(y == 0)
        def _():
            src, dst = ysum_out.at[zz, 0:2], ysum_in.at[zz, 0:2]
            remote(src, dst, ysem_s.at[zz], ysem_r.at[zz], ctx=ypart).wait_recv()

    def way(zz):
        ahead = (zz - z + NZ) % NZ
        up = (ahead <= reach[1]).astype(jnp.int32)
        return up, jnp.where(up == 1, ahead, NZ - ahead)

    def sum_hop(zz, up, at):
        return remote(
            sum_out.at[zz], sum_in.at[up, at], ssend.at[zz], srecv.at[up, at],
            ctx=jnp.where(up == 1, up_dev, down_dev),
        )

    def sum_home(zz, up, at):
        return remote(
            sum_out.at[zz], home_in.at[up, at], ssend.at[zz], homer.at[up, at],
            ctx=ctx_of(y, zz, core),
        )

    def merge(zz, up, a):
        limit = jnp.where(up == 1, reach[1], reach[0])

        @pl.when(a < limit)
        def _():
            sum_hop(zz, up, a).wait_recv()
            sum_out[zz] = (acc[y, zz] + sum_in[up, a].astype(F32)).astype(BF)

        @pl.when(a == limit)
        def _():
            sum_out[zz] = acc[y, zz].astype(BF)

    def pass_far(zz):
        up, a = way(zz)
        merge(zz, up, a)
        sum_hop(zz, up, a - 1).start()

    def pass_mid(zz):
        up, a = way(zz)
        merge(zz, up, a)
        sum_home(zz, up, a).start()

    def pass_near(zz):
        up, a = way(zz)
        sum_out[zz] = acc[y, zz].astype(BF)
        sum_home(zz, up, a).start()

    def send_across(n):
        w = pair_at(n)
        for zz in (2 * w, 2 * w + 1):
            ysum_out[zz] = acc[1 - y, zz].astype(BF)
            sum_across(zz, lambda copy: copy.start())

    def add_across(zz):
        sum_across_wait(zz)
        acc[y, zz, 0:2] += ysum_in[zz, 0:2].astype(F32)

        @pl.when(y == 1)
        def _():
            acc[y, zz, 2:4] += ysum_in[zz, 2:4].astype(F32)

    def far_near(n):
        w = pair_at(n)
        first = 2 * w
        _, da = way(first)
        _, db = way(first + 1)
        flip = (da < db).astype(jnp.int32)
        return first + flip, first + 1 - flip

    def weight_copies(step):
        peer = (tp + step) % TP
        out = []
        for n, ref in enumerate((wk, wv)):
            rows = pl.ds(pl.multiple_of(peer * FEAT + core * HALF_FEAT, 64), HALF_FEAT)
            mine = pl.ds(pl.multiple_of(core * HALF_FEAT, 64), HALF_FEAT)
            out.append(
                remote(
                    ref.at[rows, :], wbuf.at[tp, n, mine, :],
                    wsend.at[step, n], wrecv.at[step, n], tp=peer, ctx=jnp.where(step % 2 == 1, ypart, i),
                )
            )
        return out

    def weight_forwards(step):
        giver = (tp + TP - step) % TP
        out = []
        for n in range(2):
            mine = pl.ds(pl.multiple_of(core * HALF_FEAT, 64), HALF_FEAT)
            block = wbuf.at[giver, n, mine, :]
            out.append(remote(block, block, fsend.at[step, n], frecv.at[step, n], ctx=mate))
        return out

    def half_step(x, _):
        n = x // 2
        w = pair_at(n)
        far = jnp.where(x < 6, x % 2, 1 - x % 2)
        yp = (y + far) % 2

        @pl.when(far == 1)
        def _():
            across_wait(2 * w)
            across_wait(2 * w + 1)

        @pl.when(x < 7)
        def _():
            for copy in weight_copies(x + 1):
                copy.start()

        unit(yp, w, 0, 1, False)

        for at, d in ((0, 2), (3, 4)):

            @pl.when(x == at)
            def _():
                pump(d)

        @pl.when(x == 7)
        def _():
            further, _ = far_near(2)
            add_across(further)
            pass_far(further)

        own = jnp.logical_and(far == 0, n == 0)

        @pl.when(own)
        def _():
            def masked_unit(hl, _):
                unit(yp, w, hl, hl, True)
                return 0

            lax.fori_loop(0, 2, masked_unit, 0)

        @pl.when(jnp.logical_not(own))
        def _():
            hl = jnp.where(yp * NZ + 2 * w < chip, 0, 1)
            unit(yp, w, hl, hl, False)

        @pl.when(far == 1)
        def _():
            send_across(n)

        @pl.when(x == 1)
        def _():
            pump(3)

        @pl.when(x == 3)
        def _():
            add_across(2 * quad)
            add_across(2 * quad + 1)
            pass_near(2 * quad + 1 - odd)

        @pl.when(x == 5)
        def _():
            for zz in far_near(1):
                add_across(zz)
                pass_near(zz)

        @pl.when(x > 1)
        def _():
            for copy in weight_copies(x - 1):
                copy.wait_recv()
            for copy in weight_forwards(x - 1):
                copy.start()

        return 0

    lax.fori_loop(0, 8, half_step, 0)

    _, nearer = far_near(2)
    add_across(nearer)
    pass_far(nearer)
    dqs[...] = (dqa[other] * SCALE).astype(BF)
    dq_copy = remote(dqs, dqr, dsem.at[0], dsem.at[1], ctx=mate)
    dq_copy.start()
    for copy in weight_copies(TP - 1):
        copy.wait_recv()
    for copy in weight_forwards(TP - 1):
        copy.start()
    for zz in far_near(3):
        add_across(zz)
        pass_mid(zz)
    dq_copy.wait()
    for h in range(8):
        cols = slice(h * 128, (h + 1) * 128)
        low = (dqa[core, 0, cols, :] * SCALE + dqr[0, cols, :].astype(F32)).astype(BF)
        high = (dqa[core, 1, cols, :] * SCALE + dqr[1, cols, :].astype(F32)).astype(BF)
        dq_out[0:SPAN, cols] = jnp.where(flip16, high, low)
        dq_out[SPAN:, cols] = jnp.where(flip16, low, high)

    def take(up, a):
        sum_home(z, up, a).wait_recv()
        acc[y, z] += home_in[up, a].astype(F32)

    for up, a in ((0, 1), (1, 1), (0, 2), (1, 2), (odd, 3)):
        take(up, a)
    for out, at, factor in ((dk_out, 0, SCALE), (dv_out, 1, 1.0)):
        low = (acc[y, z, at] * factor).T.astype(BF)
        high = (acc[y, z, at + 2] * factor).T.astype(BF)
        cols = slice(at * 128, (at + 1) * 128)
        for rows, value in (
            (slice(0, SPAN), jnp.where(flip16, high, low)),
            (slice(SPAN, 2 * SPAN), jnp.where(flip16, low, high)),
        ):
            out[rows, :] = value
            dkv[rows, cols] = value

    def spread(step):
        return remote(dkv, gathered.at[tp], tsend.at[step], trecv.at[step], tp=(tp + step) % TP)

    for step in range(1, TP):
        spread(step).start()

    mine = dkv[...]
    loads[6].wait()

    def rows_of(yp, zz, k):
        return pl.ds(pl.multiple_of(((yp * NZ + zz) * 2 + k) * WROWS, 32), WROWS)

    def swap_part(yp):
        return remote(cs.at[yp], cr.at[yp], csend.at[yp], crecv.at[yp], ctx=mate)

    for turn in range(2):
        yp = (1 - y) if turn == 0 else y
        for n in range(5):
            at = pl.ds(pl.multiple_of(yp * 2560 + n * 512, 512), 512)
            part[at, :] = dot(hid[:, at], mine, TN)

        def fill(zz, _):
            cs[yp, zz] = part[rows_of(yp, zz, other), :].astype(BF)
            return 0

        lax.fori_loop(0, NZ, fill, 0)
        swap_part(yp).start()
    def own_part(yp, zz):
        return part[rows_of(yp, zz, core), :] + cr[yp, zz].astype(F32)

    def arm(up, a, yp):
        return remote(
            gout.at[up, a, yp], gin.at[up, a - 1, yp],
            gsend.at[up, a, yp], grecv.at[up, a - 1, yp],
            ctx=up_dev if up else down_dev,
        )

    def arms(k, _):
        a = 4 - k
        for turn in range(2):
            yp = (1 - y) if turn == 0 else y

            @pl.when(k == 0)
            def _():
                swap_part(yp).wait()

            for up in (1, 0):
                zz = (z + a) % NZ if up else (z - a + NZ) % NZ

                @pl.when(a == reach[up])
                def _():
                    gout[up, a, yp] = own_part(yp, zz).astype(BF)

                @pl.when(a < reach[up])
                def _():
                    arm(up, a + 1, yp).wait_recv()
                    gout[up, a, yp] = (own_part(yp, zz) + gin[up, a, yp].astype(F32)).astype(BF)

                @pl.when(a <= reach[up])
                def _():
                    arm(up, a, yp).start()

        return 0

    lax.fori_loop(0, 4, arms, 0)

    def plane_sum(yp):
        arm(1, 1, yp).wait_recv()
        arm(0, 1, yp).wait_recv()
        return own_part(yp, z) + gin[1, 0, yp].astype(F32) + gin[0, 0, yp].astype(F32)

    fs[...] = plane_sum(1 - y).astype(BF)
    f_copy = remote(fs, fr, dsem.at[2], dsem.at[3], ctx=ypart)
    f_copy.start()
    final = plane_sum(y)

    gathered[tp] = mine
    loads[7].wait()
    loads[8].wait()
    for step in range(1, TP):
        for copy in weight_forwards(step):
            copy.wait()
        spread(step).wait_recv()
    total = None
    for giver in range(TP):
        got = gathered[giver]
        term = dot(got[:, :128], wbuf[giver, 0], NT) + dot(got[:, 128:], wbuf[giver, 1], NT)
        total = term if total is None else total + term
    dh_out[...] = total.astype(BF)

    f_copy.wait()
    final = final + fr[...].astype(F32)
    gk_out[...] = final[:, :128]
    gv_out[...] = final[:, 128:]

    def drain(s, _):
        across(s, lambda copy: copy.wait_send())
        sum_across(s, lambda copy: copy.wait_send())

        @pl.when(s > 0)
        def _():
            for copy in weight_copies(s):
                copy.wait_send()
            sum_hop(z_at(s), 0, 0).wait_send()
            spread(s).wait_send()

        for up in (0, 1):

            @pl.when(s < reach[up])
            def _():
                hop(up, s).wait_send()
                for yp in range(2):
                    arm(up, s + 1, yp).wait_send()

        return 0

    lax.fori_loop(0, NZ, drain, 0)


def backward(*args):
    vmem = pl.BlockSpec(memory_space=pltpu.VMEM)
    hbm = pl.BlockSpec(memory_space=pl.ANY)
    dma = pltpu.SemaphoreType.DMA
    sds = jax.ShapeDtypeStruct
    rows = (2, 2, 1024, 128)
    block = (4, 128, 128)
    piece = (WROWS, 256)
    return pl.pallas_call(
        kernel,
        out_shape=[
            sds((256, 1024), BF),
            sds((256, 128), BF),
            sds((256, 128), BF),
            sds((WROWS, 128), F32),
            sds((WROWS, 128), F32),
            sds((256, FEAT), BF),
        ],
        in_specs=[pl.BlockSpec(memory_space=pltpu.SMEM)] + [hbm] * 9,
        out_specs=[vmem] * 6,
        scratch_shapes=[
            pltpu.VMEM((256, 1024), BF),
            pltpu.VMEM((256, 128), BF),
            pltpu.VMEM((256, 128), BF),
            pltpu.VMEM((256, 1024), BF),
            pltpu.VMEM((256, 1024), BF),
            pltpu.VMEM((8, 256), F32),
            pltpu.VMEM((256, 5120), BF),
            pltpu.VMEM(rows, BF),
            pltpu.VMEM(rows, BF),
            pltpu.VMEM(rows, BF),
            pltpu.VMEM((2, 2, 8, 128), F32),
            pltpu.VMEM(rows, F32),
            pltpu.VMEM(rows, F32),
            pltpu.VMEM(rows, F32),
            pltpu.VMEM((2, NZ) + block, BF),
            pltpu.VMEM((2, NZ) + block, F32),
            pltpu.VMEM((NZ,) + block, BF),
            pltpu.VMEM((NZ,) + block, BF),
            pltpu.VMEM((NZ,) + block, BF),
            pltpu.VMEM((2, 4) + block, BF),
            pltpu.VMEM((2, 4) + block, BF),
            pltpu.VMEM((2, 1024, 128), BF),
            pltpu.VMEM((2, 1024, 128), BF),
            pltpu.VMEM((TP, 2, FEAT, 128), BF),
            pltpu.VMEM((256, 256), BF),
            pltpu.VMEM((TP, 256, 256), BF),
            pltpu.VMEM((5120, 256), F32),
            pltpu.VMEM((2, NZ) + piece, BF),
            pltpu.VMEM((2, NZ) + piece, BF),
            pltpu.VMEM((2, 5, 2) + piece, BF),
            pltpu.VMEM((2, 4, 2) + piece, BF),
            pltpu.VMEM(piece, BF),
            pltpu.VMEM(piece, BF),
            dma((9,)),
            dma((4,)),
            dma((4,)),
            dma((2, 5)),
            dma((2, 5)),
            dma((NZ,)),
            dma((NZ,)),
            dma((NZ,)),
            dma((NZ,)),
            dma((NZ,)),
            dma((2, 4)),
            dma((2, 4)),
            dma((TP, 2)),
            dma((TP, 2)),
            dma((TP, 2)),
            dma((TP, 2)),
            dma((4,)),
            dma((TP,)),
            dma((TP,)),
            dma((2,)),
            dma((2,)),
            dma((2, 5, 2)),
            dma((2, 5, 2)),
        ],
        compiler_params=pltpu.CompilerParams(
            collective_id=0, has_side_effects=True, vmem_limit_bytes=58 * 2**20
        ),
        cost_estimate=pl.CostEstimate(
            flops=12 * 10**9, bytes_accessed=10**7, transcendentals=9 * 10**6
        ),
    )(*args)


def copy_kernel(*refs):
    sems = refs[18]
    inward = [pltpu.make_async_copy(refs[n], refs[12 + n], sems.at[0, n]) for n in range(6)]
    outward = [pltpu.make_async_copy(refs[12 + n], refs[6 + n], sems.at[1, n]) for n in range(6)]
    for copy in inward:
        copy.start()
    for n in range(6):
        inward[n].wait()
        outward[n].start()
    for copy in outward:
        copy.wait()


def place_outputs(*outs):
    hbm = pl.BlockSpec(memory_space=pl.ANY)
    return pl.pallas_call(
        copy_kernel,
        out_shape=[jax.ShapeDtypeStruct(a.shape, a.dtype) for a in outs],
        in_specs=[hbm] * 6,
        out_specs=[hbm] * 6,
        scratch_shapes=[pltpu.VMEM(a.shape, a.dtype) for a in outs]
        + [pltpu.SemaphoreType.DMA((2, 6))],
        compiler_params=pltpu.CompilerParams(vmem_limit_bytes=60 * 2**20),
    )(*outs)


def shards(q, k, v, o, d, ln, order, hidden, wk, wv):
    return tuple(place_outputs(*backward(order, q, k, v, o, d, ln, hidden, wk, wv)))


def solution(mesh):
    split = P("ctx", "tp")
    in_specs = (split,) * 5 + (P("tp", "ctx"), P(), P("ctx", None), P(None, "tp"), P(None, "tp"))
    return jax.shard_map(
        shards, mesh=mesh, in_specs=in_specs, out_specs=(split,) * 6, check_vma=False
    )
```

```python
import functools
import math

import jax
import jax.numpy as jnp
from jax import lax
from jax.experimental import pallas as pl
from jax.experimental.pallas import tpu as pltpu
from jax.sharding import PartitionSpec as P

BF = jnp.bfloat16
F32 = jnp.float32
MESH = pl.DeviceIdType.MESH
SCALE = 1.0 / math.sqrt(128)
LOG2E = math.log2(math.e)
NT = (((1,), (1,)), ((), ()))
TN = (((0,), (0,)), ((), ()))
SPAN = 128
TP = 8
NZ = 8
FEAT = 640
HALF_FEAT = 320
WROWS = 160

dot = functools.partial(lax.dot_general, preferred_element_type=F32)


def mm(a, b):
    return jnp.dot(a, b, preferred_element_type=F32)


def place():
    i = lax.axis_index("ctx")
    return i, i % 2, (i // 2) % NZ, i // 16


def ctx_of(y, z, core):
    return y * 16 + z * 2 + core


def remote(src, dst, send, recv, **where):
    return pltpu.make_async_remote_copy(
        src_ref=src, dst_ref=dst, send_sem=send, recv_sem=recv, device_id=where, device_id_type=MESH
    )


def kernel(
    order, q_hbm, k_hbm, v_hbm, o_hbm, d_hbm, ln_hbm, hid_hbm, wk, wv,
    dq_out, dk_out, dv_out, gk_out, gv_out, dh_out,
    q_in, k_in, v_in, o_in, d_in, ln_in, hid,
    qb, db, ob, terms, lnb, deb, dqa, kv, acc, ysum_out, ysum_in, sum_out, sum_in, home_in, dqs, dqr,
    wbuf, dkv, gathered, part, cs, cr, gout, gin, fs, fr,
    lsem, xsend, xrecv, zsend, zrecv, ysend, yrecv, ysem_s, ysem_r, ssend, srecv, homer,
    wsend, wrecv, fsend, frecv, dsem, tsend, trecv, csend, crecv, gsend, grecv,
):
    i, core, z, y = place()
    tp = lax.axis_index("tp")
    other = 1 - core
    chip = y * NZ + z
    odd = z % 2
    quad = z // 2
    ypart = ctx_of(1 - y, z, core)
    mate = ctx_of(y, z, other)

    def z_at(step):
        return (z + step + NZ) % NZ

    up_dev = ctx_of(y, z_at(1), core)
    down_dev = ctx_of(y, z_at(-1), core)
    reach = (3 + core, 4 - core)

    loads = [
        pltpu.make_async_copy(src, dst, lsem.at[n])
        for n, (src, dst) in enumerate(
            (
                (k_hbm, k_in), (v_hbm, v_in), (q_hbm, q_in), (d_hbm, d_in), (o_hbm, o_in),
                (ln_hbm, ln_in), (hid_hbm, hid),
                (wk.at[pl.ds(pl.multiple_of(tp * FEAT, FEAT), FEAT), :], wbuf.at[tp, 0]),
                (wv.at[pl.ds(pl.multiple_of(tp * FEAT, FEAT), FEAT), :], wbuf.at[tp, 1]),
            )
        )
    ]
    for load in loads:
        load.start()

    barrier = pltpu.get_barrier_semaphore()
    for dev in (ypart, mate):
        pl.semaphore_signal(barrier, inc=1, device_id={"ctx": dev}, device_id_type=MESH)
    for step in range(1, NZ):
        dev = ctx_of(y, z_at(step), core)
        pl.semaphore_signal(barrier, inc=1, device_id={"ctx": dev}, device_id_type=MESH)
        peer = (tp + step) % TP
        pl.semaphore_signal(barrier, inc=1, device_id={"tp": peer}, device_id_type=MESH)
        if step % 2:
            pl.semaphore_signal(
                barrier, inc=1, device_id={"ctx": ypart, "tp": peer}, device_id_type=MESH
            )

    flip8 = jnp.full((8, 128), order[2 * i], jnp.int32) != jnp.full((8, 128), i, jnp.int32)
    flip_wide = jnp.concatenate([jnp.where(flip8, 1.0, 0.0)] * 16, axis=0)
    flip16 = flip_wide.astype(BF) > 0.5

    def canon(first, second, hl):
        return jnp.where(flip16, second, first) if hl == 0 else jnp.where(flip16, first, second)

    loads[0].wait()
    loads[1].wait()
    for hl in range(2):
        kv[y, z, 2 * hl] = canon(k_in[:SPAN, :], k_in[SPAN:, :], hl)
        kv[y, z, 2 * hl + 1] = canon(v_in[:SPAN, :], v_in[SPAN:, :], hl)
    pl.semaphore_wait(barrier, 2 * NZ + TP // 2)

    def hop(up, d):
        block = kv.at[y, z_at(-d if up else d)]
        return remote(
            block, block, zsend.at[up, d], zrecv.at[up, d + 1], ctx=up_dev if up else down_dev
        )

    def across(zz, act):
        @pl.when(y == 0)
        def _():
            block = kv.at[0, zz, 0:2]
            act(remote(block, block, ysend.at[zz], yrecv.at[zz], ctx=ypart))

        @pl.when(y == 1)
        def _():
            block = kv.at[1, zz]
            act(remote(block, block, ysend.at[zz], yrecv.at[zz], ctx=ypart))

    def across_wait(zz):
        @pl.when(y == 1)
        def _():
            block = kv.at[0, zz, 0:2]
            remote(block, block, ysend.at[zz], yrecv.at[zz], ctx=ypart).wait_recv()

        @pl.when(y == 0)
        def _():
            block = kv.at[1, zz]
            remote(block, block, ysend.at[zz], yrecv.at[zz], ctx=ypart).wait_recv()

    hop(1, 0).start()
    hop(0, 0).start()
    across(z, lambda copy: copy.start())

    for load in loads[2:6]:
        load.wait()
    for hl in range(2):
        for h in range(8):
            cols = slice(h * 128, (h + 1) * 128)
            for full, here in ((qb, q_in), (db, d_in)):
                full[core, hl, cols, :] = canon(here[:SPAN, cols], here[SPAN:, cols], hl)
            ob[hl, cols, :] = canon(o_in[:SPAN, cols], o_in[SPAN:, cols], hl)
    swaps = [
        remote(ref.at[core], ref.at[core], xsend.at[n], xrecv.at[n], ctx=mate)
        for n, ref in enumerate((qb, db, terms))
    ]
    swaps[0].start()
    swaps[1].start()
    both = ln_in[...] * LOG2E
    terms[core, 0, 0] = jnp.where(flip8, both[:, SPAN:], both[:, :SPAN])
    terms[core, 1, 0] = jnp.where(flip8, both[:, :SPAN], both[:, SPAN:])
    ones = jnp.ones((16, 128), BF)
    head = lax.broadcasted_iota(jnp.int32, (8, 128), 0)
    for hl in range(2):
        prod = db[core, hl].astype(F32) * ob[hl].astype(F32)
        high = prod.astype(BF)
        low = (prod - high.astype(F32)).astype(BF)
        flat = (dot(ones, high, NT) + dot(ones, low, NT))[:8, :]
        delta = flat[:, 0:128]
        for h in range(1, 8):
            delta = jnp.where(head == h, flat[:, h * 128 : (h + 1) * 128], delta)
        terms[core, hl, 1] = delta
    swaps[2].start()

    def zero(n, _):
        for at in range(4):
            acc[n // NZ, n % NZ, at] = jnp.zeros((128, 128), F32)
        return 0

    lax.fori_loop(0, 2 * NZ, zero, 0)
    dqa[...] = jnp.zeros_like(dqa)

    head_of = lax.broadcasted_iota(jnp.int32, (32, 1024), 1) // 128
    pick = (lax.broadcasted_iota(jnp.int32, (32, 1024), 0) % 8 == head_of).astype(F32).astype(BF)

    def row_terms(slot):
        for hl in range(2):
            for at, wide_ref in ((0, lnb), (1, deb)):
                term = terms[slot, hl, at]
                p1 = term.astype(BF)
                rest = term - p1.astype(F32)
                p2 = rest.astype(BF)
                rest = rest - p2.astype(F32)
                p3 = rest.astype(BF)
                parts = jnp.concatenate(
                    [p1.astype(F32), p2.astype(F32), p3.astype(F32), jnp.zeros((8, 128), F32)],
                    axis=0,
                ).astype(BF)
                wide = dot(parts, pick, TN)
                for h in range(8):
                    cols = slice(h * 128, (h + 1) * 128)
                    wide_ref[slot, hl, cols, :] = wide[:, cols]

    row_terms(core)

    def pump(d):
        for up in (1, 0):

            @pl.when(d <= reach[up])
            def _():
                hop(up, d - 1).wait_recv()

                @pl.when(d < reach[up])
                def _():
                    hop(up, d).start()

                across(z_at(-d if up else d), lambda copy: copy.start())

    pump(1)
    for swap in swaps:
        swap.wait()
    row_terms(other)

    def unit(yp, w, hk, hq, masked):
        ra = 2 * w
        rb = 2 * w + 1
        k = jnp.concatenate([kv[yp, ra, 2 * hk], kv[yp, rb, 2 * hk]], axis=0)
        v = jnp.concatenate([kv[yp, ra, 2 * hk + 1], kv[yp, rb, 2 * hk + 1]], axis=0)
        gk = None
        gv = None
        for slot in range(2):
            q = qb[slot, hq]
            d = db[slot, hq]
            ln = lnb[slot, hq]
            de = deb[slot, hq]
            scores = dot(q, k, NT)
            dp = dot(d, v, NT)
            prob = jnp.exp2(scores * (SCALE * LOG2E) - jnp.concatenate([ln, ln], axis=1))
            if masked:
                qi = 2 * chip + slot
                qspan = jnp.where(hq == 0, qi, 63 - qi)
                shape = (1024, 128)
                gap = (
                    lax.broadcasted_iota(jnp.int32, shape, 0) % SPAN
                    - lax.broadcasted_iota(jnp.int32, shape, 1)
                )
                seen = []
                for rk in (ra, rb):
                    ki = 2 * (yp * NZ + rk) + core
                    kspan = jnp.where(hk == 0, ki, 63 - ki)
                    seen.append(gap >= (kspan - qspan) * SPAN)
                prob = jnp.concatenate(
                    [
                        jnp.where(seen[0], prob[:, :128], 0.0),
                        jnp.where(seen[1], prob[:, 128:], 0.0),
                    ],
                    axis=1,
                )
            ds = (prob * (dp - jnp.concatenate([de, de], axis=1))).astype(BF)
            pr = prob.astype(BF)
            dqa[slot, hq] += mm(ds, k)
            gk = dot(q, ds, TN) if gk is None else gk + dot(q, ds, TN)
            gv = dot(d, pr, TN) if gv is None else gv + dot(d, pr, TN)
        acc[yp, ra, 2 * hk] += gk[:, :128]
        acc[yp, rb, 2 * hk] += gk[:, 128:]
        acc[yp, ra, 2 * hk + 1] += gv[:, :128]
        acc[yp, rb, 2 * hk + 1] += gv[:, 128:]

    def pair_at(n):
        side = jnp.where(n == 1, 2 * odd - 1, 1 - 2 * odd)
        return (quad + jnp.where(n == 0, 0, jnp.where(n == 2, 2, side)) + 4) % 4

    def sum_across(zz, act):
        @pl.when(y == 0)
        def _():
            act(remote(ysum_out.at[zz], ysum_in.at[zz], ysem_s.at[zz], ysem_r.at[zz], ctx=ypart))

        @pl.when(y == 1)
        def _():
            src, dst = ysum_out.at[zz, 0:2], ysum_in.at[zz, 0:2]
            act(remote(src, dst, ysem_s.at[zz], ysem_r.at[zz], ctx=ypart))

    def sum_across_wait(zz):
        @pl.when(y == 1)
        def _():
            remote(
                ysum_out.at[zz], ysum_in.at[zz], ysem_s.at[zz], ysem_r.at[zz], ctx=ypart
            ).wait_recv()

        @pl.when(y == 0)
        def _():
            src, dst = ysum_out.at[zz, 0:2], ysum_in.at[zz, 0:2]
            remote(src, dst, ysem_s.at[zz], ysem_r.at[zz], ctx=ypart).wait_recv()

    def way(zz):
        ahead = (zz - z + NZ) % NZ
        up = (ahead <= reach[1]).astype(jnp.int32)
        return up, jnp.where(up == 1, ahead, NZ - ahead)

    def sum_hop(zz, up, at):
        return remote(
            sum_out.at[zz], sum_in.at[up, at], ssend.at[zz], srecv.at[up, at],
            ctx=jnp.where(up == 1, up_dev, down_dev),
        )

    def sum_home(zz, up, at):
        return remote(
            sum_out.at[zz], home_in.at[up, at], ssend.at[zz], homer.at[up, at],
            ctx=ctx_of(y, zz, core),
        )

    def merge(zz, up, a):
        limit = jnp.where(up == 1, reach[1], reach[0])

        @pl.when(a < limit)
        def _():
            sum_hop(zz, up, a).wait_recv()
            sum_out[zz] = (acc[y, zz] + sum_in[up, a].astype(F32)).astype(BF)

        @pl.when(a == limit)
        def _():
            sum_out[zz] = acc[y, zz].astype(BF)

    def pass_far(zz):
        up, a = way(zz)
        merge(zz, up, a)
        sum_hop(zz, up, a - 1).start()

    def pass_mid(zz):
        up, a = way(zz)
        merge(zz, up, a)
        sum_home(zz, up, a).start()

    def pass_near(zz):
        up, a = way(zz)
        sum_out[zz] = acc[y, zz].astype(BF)
        sum_home(zz, up, a).start()

    def send_across(n):
        for zz in far_near(n):
            ysum_out[zz] = acc[1 - y, zz].astype(BF)
            sum_across(zz, lambda copy: copy.start())

    def add_across(zz):
        sum_across_wait(zz)
        acc[y, zz, 0:2] += ysum_in[zz, 0:2].astype(F32)

        @pl.when(y == 1)
        def _():
            acc[y, zz, 2:4] += ysum_in[zz, 2:4].astype(F32)

    def far_near(n):
        w = pair_at(n)
        first = 2 * w
        _, da = way(first)
        _, db = way(first + 1)
        flip = (da < db).astype(jnp.int32)
        return first + flip, first + 1 - flip

    def weight_copies(step):
        peer = (tp + step) % TP
        out = []
        for n, ref in enumerate((wk, wv)):
            rows = pl.ds(pl.multiple_of(peer * FEAT + core * HALF_FEAT, 64), HALF_FEAT)
            mine = pl.ds(pl.multiple_of(core * HALF_FEAT, 64), HALF_FEAT)
            out.append(
                remote(
                    ref.at[rows, :], wbuf.at[tp, n, mine, :],
                    wsend.at[step, n], wrecv.at[step, n], tp=peer, ctx=jnp.where(step % 2 == 1, ypart, i),
                )
            )
        return out

    def weight_forwards(step):
        giver = (tp + TP - step) % TP
        out = []
        for n in range(2):
            mine = pl.ds(pl.multiple_of(core * HALF_FEAT, 64), HALF_FEAT)
            block = wbuf.at[giver, n, mine, :]
            out.append(remote(block, block, fsend.at[step, n], frecv.at[step, n], ctx=mate))
        return out

    def half_step(x, _):
        n = x // 2
        w = pair_at(n)
        far = jnp.where(x < 6, x % 2, 1 - x % 2)
        yp = (y + far) % 2

        @pl.when(far == 1)
        def _():
            across_wait(2 * w)
            across_wait(2 * w + 1)

        @pl.when(x < 7)
        def _():
            for copy in weight_copies(x + 1):
                copy.start()

        unit(yp, w, 0, 1, False)

        for at, d in ((0, 2), (3, 4)):

            @pl.when(x == at)
            def _():
                pump(d)

        @pl.when(x == 7)
        def _():
            further, _ = far_near(2)
            add_across(further)
            pass_far(further)

        own = jnp.logical_and(far == 0, n == 0)

        @pl.when(own)
        def _():
            def masked_unit(hl, _):
                unit(yp, w, hl, hl, True)
                return 0

            lax.fori_loop(0, 2, masked_unit, 0)

        @pl.when(jnp.logical_not(own))
        def _():
            hl = jnp.where(yp * NZ + 2 * w < chip, 0, 1)
            unit(yp, w, hl, hl, False)

        @pl.when(far == 1)
        def _():
            send_across(n)

        @pl.when(x == 1)
        def _():
            pump(3)

        @pl.when(x == 3)
        def _():
            add_across(2 * quad)
            add_across(2 * quad + 1)
            pass_near(2 * quad + 1 - odd)

        @pl.when(x == 5)
        def _():
            for zz in far_near(1):
                add_across(zz)
                pass_near(zz)

        @pl.when(x > 1)
        def _():
            for copy in weight_copies(x - 1):
                copy.wait_recv()
            for copy in weight_forwards(x - 1):
                copy.start()

        return 0

    lax.fori_loop(0, 8, half_step, 0)

    _, nearer = far_near(2)
    add_across(nearer)
    pass_far(nearer)
    dqs[...] = (dqa[other] * SCALE).astype(BF)
    dq_copy = remote(dqs, dqr, dsem.at[0], dsem.at[1], ctx=mate)
    dq_copy.start()
    for copy in weight_copies(TP - 1):
        copy.wait_recv()
    for copy in weight_forwards(TP - 1):
        copy.start()
    for zz in far_near(3):
        add_across(zz)
        pass_mid(zz)
    dq_copy.wait()
    for h in range(8):
        cols = slice(h * 128, (h + 1) * 128)
        low = (dqa[core, 0, cols, :] * SCALE + dqr[0, cols, :].astype(F32)).astype(BF)
        high = (dqa[core, 1, cols, :] * SCALE + dqr[1, cols, :].astype(F32)).astype(BF)
        dq_out[0:SPAN, cols] = jnp.where(flip16, high, low)
        dq_out[SPAN:, cols] = jnp.where(flip16, low, high)

    def take(up, a):
        sum_home(z, up, a).wait_recv()
        acc[y, z] += home_in[up, a].astype(F32)

    for up, a in ((0, 1), (1, 1), (0, 2), (1, 2), (odd, 3)):
        take(up, a)
    for out, at, factor in ((dk_out, 0, SCALE), (dv_out, 1, 1.0)):
        low = (acc[y, z, at] * factor).T.astype(BF)
        high = (acc[y, z, at + 2] * factor).T.astype(BF)
        cols = slice(at * 128, (at + 1) * 128)
        for rows, value in (
            (slice(0, SPAN), jnp.where(flip16, high, low)),
            (slice(SPAN, 2 * SPAN), jnp.where(flip16, low, high)),
        ):
            out[rows, :] = value
            dkv[rows, cols] = value

    def spread(step):
        return remote(dkv, gathered.at[tp], tsend.at[step], trecv.at[step], tp=(tp + step) % TP)

    for step in range(1, TP):
        spread(step).start()

    mine = dkv[...]
    loads[6].wait()

    def rows_of(yp, zz, k):
        return pl.ds(pl.multiple_of(((yp * NZ + zz) * 2 + k) * WROWS, 32), WROWS)

    def swap_part(yp):
        return remote(cs.at[yp], cr.at[yp], csend.at[yp], crecv.at[yp], ctx=mate)

    for turn in range(2):
        yp = (1 - y) if turn == 0 else y
        for n in range(5):
            at = pl.ds(pl.multiple_of(yp * 2560 + n * 512, 512), 512)
            part[at, :] = dot(hid[:, at], mine, TN)

        def fill(zz, _):
            cs[yp, zz] = part[rows_of(yp, zz, other), :].astype(BF)
            return 0

        lax.fori_loop(0, NZ, fill, 0)
        swap_part(yp).start()
    def own_part(yp, zz, ch):
        cols = slice(ch * 128, (ch + 1) * 128)
        return part[rows_of(yp, zz, core), cols] + cr[yp, zz, :, cols].astype(F32)

    def arm(up, a, q):
        return remote(
            gout.at[up, a, q], gin.at[up, a - 1, q],
            gsend.at[up, a, q], grecv.at[up, a - 1, q],
            ctx=up_dev if up else down_dev,
        )

    def arms(k, _):
        a = 4 - k
        for turn in range(2):
            yp = (1 - y) if turn == 0 else y

            @pl.when(k == 0)
            def _():
                swap_part(yp).wait()

            for ch in range(2):
                q = yp * 2 + ch
                for up in (1, 0):
                    zz = (z + a) % NZ if up else (z - a + NZ) % NZ

                    @pl.when(a == reach[up])
                    def _():
                        gout[up, a, q] = own_part(yp, zz, ch).astype(BF)

                    @pl.when(a < reach[up])
                    def _():
                        arm(up, a + 1, q).wait_recv()
                        mix = own_part(yp, zz, ch) + gin[up, a, q].astype(F32)
                        gout[up, a, q] = mix.astype(BF)

                    @pl.when(a <= reach[up])
                    def _():
                        arm(up, a, q).start()

        return 0

    lax.fori_loop(0, 4, arms, 0)

    def plane_sum(yp, ch):
        q = yp * 2 + ch
        arm(1, 1, q).wait_recv()
        arm(0, 1, q).wait_recv()
        return own_part(yp, z, ch) + gin[1, 0, q].astype(F32) + gin[0, 0, q].astype(F32)

    f_copies = []
    for ch in range(2):
        fs[ch] = plane_sum(1 - y, ch).astype(BF)
        f_copies.append(
            remote(fs.at[ch], fr.at[ch], dsem.at[2 + 2 * ch], dsem.at[3 + 2 * ch], ctx=ypart)
        )
        f_copies[ch].start()

    gathered[tp] = mine
    loads[7].wait()
    loads[8].wait()
    for step in range(1, TP):
        for copy in weight_forwards(step):
            copy.wait()
        spread(step).wait_recv()
    total = None
    for giver in range(TP):
        got = gathered[giver]
        term = dot(got[:, :128], wbuf[giver, 0], NT) + dot(got[:, 128:], wbuf[giver, 1], NT)
        total = term if total is None else total + term
    dh_out[...] = total.astype(BF)

    for ch, out in ((0, gk_out), (1, gv_out)):
        mine_sum = plane_sum(y, ch)
        f_copies[ch].wait()
        out[...] = mine_sum + fr[ch].astype(F32)

    def drain(s, _):
        across(s, lambda copy: copy.wait_send())
        sum_across(s, lambda copy: copy.wait_send())

        @pl.when(s > 0)
        def _():
            for copy in weight_copies(s):
                copy.wait_send()
            sum_hop(z_at(s), 0, 0).wait_send()
            spread(s).wait_send()

        for up in (0, 1):

            @pl.when(s < reach[up])
            def _():
                hop(up, s).wait_send()
                for q in range(4):
                    arm(up, s + 1, q).wait_send()

        return 0

    lax.fori_loop(0, NZ, drain, 0)


def backward(*args):
    vmem = pl.BlockSpec(memory_space=pltpu.VMEM)
    hbm = pl.BlockSpec(memory_space=pl.ANY)
    dma = pltpu.SemaphoreType.DMA
    sds = jax.ShapeDtypeStruct
    rows = (2, 2, 1024, 128)
    block = (4, 128, 128)
    piece = (WROWS, 256)
    return pl.pallas_call(
        kernel,
        out_shape=[
            sds((256, 1024), BF),
            sds((256, 128), BF),
            sds((256, 128), BF),
            sds((WROWS, 128), F32),
            sds((WROWS, 128), F32),
            sds((256, FEAT), BF),
        ],
        in_specs=[pl.BlockSpec(memory_space=pltpu.SMEM)] + [hbm] * 9,
        out_specs=[vmem] * 6,
        scratch_shapes=[
            pltpu.VMEM((256, 1024), BF),
            pltpu.VMEM((256, 128), BF),
            pltpu.VMEM((256, 128), BF),
            pltpu.VMEM((256, 1024), BF),
            pltpu.VMEM((256, 1024), BF),
            pltpu.VMEM((8, 256), F32),
            pltpu.VMEM((256, 5120), BF),
            pltpu.VMEM(rows, BF),
            pltpu.VMEM(rows, BF),
            pltpu.VMEM((2, 1024, 128), BF),
            pltpu.VMEM((2, 2, 2, 8, 128), F32),
            pltpu.VMEM(rows, F32),
            pltpu.VMEM(rows, F32),
            pltpu.VMEM(rows, F32),
            pltpu.VMEM((2, NZ) + block, BF),
            pltpu.VMEM((2, NZ) + block, F32),
            pltpu.VMEM((NZ,) + block, BF),
            pltpu.VMEM((NZ,) + block, BF),
            pltpu.VMEM((NZ,) + block, BF),
            pltpu.VMEM((2, 4) + block, BF),
            pltpu.VMEM((2, 4) + block, BF),
            pltpu.VMEM((2, 1024, 128), BF),
            pltpu.VMEM((2, 1024, 128), BF),
            pltpu.VMEM((TP, 2, FEAT, 128), BF),
            pltpu.VMEM((256, 256), BF),
            pltpu.VMEM((TP, 256, 256), BF),
            pltpu.VMEM((5120, 256), F32),
            pltpu.VMEM((2, NZ) + piece, BF),
            pltpu.VMEM((2, NZ) + piece, BF),
            pltpu.VMEM((2, 5, 4, WROWS, 128), BF),
            pltpu.VMEM((2, 4, 4, WROWS, 128), BF),
            pltpu.VMEM((2, WROWS, 128), BF),
            pltpu.VMEM((2, WROWS, 128), BF),
            dma((9,)),
            dma((4,)),
            dma((4,)),
            dma((2, 5)),
            dma((2, 5)),
            dma((NZ,)),
            dma((NZ,)),
            dma((NZ,)),
            dma((NZ,)),
            dma((NZ,)),
            dma((2, 4)),
            dma((2, 4)),
            dma((TP, 2)),
            dma((TP, 2)),
            dma((TP, 2)),
            dma((TP, 2)),
            dma((6,)),
            dma((TP,)),
            dma((TP,)),
            dma((2,)),
            dma((2,)),
            dma((2, 5, 4)),
            dma((2, 5, 4)),
        ],
        compiler_params=pltpu.CompilerParams(
            collective_id=0, has_side_effects=True, vmem_limit_bytes=58 * 2**20
        ),
        cost_estimate=pl.CostEstimate(
            flops=12 * 10**9, bytes_accessed=10**7, transcendentals=9 * 10**6
        ),
    )(*args)


def copy_kernel(*refs):
    sems = refs[18]
    inward = [pltpu.make_async_copy(refs[n], refs[12 + n], sems.at[0, n]) for n in range(6)]
    outward = [pltpu.make_async_copy(refs[12 + n], refs[6 + n], sems.at[1, n]) for n in range(6)]
    for copy in inward:
        copy.start()
    for n in range(6):
        inward[n].wait()
        outward[n].start()
    for copy in outward:
        copy.wait()


def place_outputs(*outs):
    hbm = pl.BlockSpec(memory_space=pl.ANY)
    return pl.pallas_call(
        copy_kernel,
        out_shape=[jax.ShapeDtypeStruct(a.shape, a.dtype) for a in outs],
        in_specs=[hbm] * 6,
        out_specs=[hbm] * 6,
        scratch_shapes=[pltpu.VMEM(a.shape, a.dtype) for a in outs]
        + [pltpu.SemaphoreType.DMA((2, 6))],
        compiler_params=pltpu.CompilerParams(vmem_limit_bytes=60 * 2**20),
    )(*outs)


def shards(q, k, v, o, d, ln, order, hidden, wk, wv):
    return tuple(place_outputs(*backward(order, q, k, v, o, d, ln, hidden, wk, wv)))


def solution(mesh):
    split = P("ctx", "tp")
    in_specs = (split,) * 5 + (P("tp", "ctx"), P(), P("ctx", None), P(None, "tp"), P(None, "tp"))
    return jax.shard_map(
        shards, mesh=mesh, in_specs=in_specs, out_specs=(split,) * 6, check_vma=False
    )
```

```python
import functools
import math

import jax
import jax.numpy as jnp
from jax import lax
from jax.experimental import pallas as pl
from jax.experimental.pallas import tpu as pltpu
from jax.sharding import PartitionSpec as P

BF = jnp.bfloat16
F32 = jnp.float32
MESH = pl.DeviceIdType.MESH
SCALE = 1.0 / math.sqrt(128)
LOG2E = math.log2(math.e)
NT = (((1,), (1,)), ((), ()))
TN = (((0,), (0,)), ((), ()))
SPAN = 128
TP = 8
NZ = 8
FEAT = 640
HALF_FEAT = 320
WROWS = 160

dot = functools.partial(lax.dot_general, preferred_element_type=F32)


def mm(a, b):
    return jnp.dot(a, b, preferred_element_type=F32)


def place():
    i = lax.axis_index("ctx")
    return i, i % 2, (i // 2) % NZ, i // 16


def ctx_of(y, z, core):
    return y * 16 + z * 2 + core


def remote(src, dst, send, recv, **where):
    return pltpu.make_async_remote_copy(
        src_ref=src, dst_ref=dst, send_sem=send, recv_sem=recv, device_id=where, device_id_type=MESH
    )


def kernel(
    order, q_hbm, k_hbm, v_hbm, o_hbm, d_hbm, ln_hbm, hid_hbm, wk, wv,
    dq_out, dk_out, dv_out, gk_out, gv_out, dh_out,
    q_in, k_in, v_in, o_in, d_in, ln_in, hid,
    qb, db, ob, terms, lnb, deb, dqa, kv, acc, ysum_out, ysum_in, sum_out, sum_in, home_in, dqs, dqr,
    wbuf, dkv, gathered, part, cs, cr, gout, gin, fs, fr,
    lsem, xsend, xrecv, zsend, zrecv, ysend, yrecv, ysem_s, ysem_r, ssend, srecv, homer,
    wsend, wrecv, fsend, frecv, dsem, tsend, trecv, csend, crecv, gsend, grecv,
):
    i, core, z, y = place()
    tp = lax.axis_index("tp")
    other = 1 - core
    chip = y * NZ + z
    odd = z % 2
    quad = z // 2
    ypart = ctx_of(1 - y, z, core)
    mate = ctx_of(y, z, other)

    def z_at(step):
        return (z + step + NZ) % NZ

    up_dev = ctx_of(y, z_at(1), core)
    down_dev = ctx_of(y, z_at(-1), core)
    reach = (3 + core, 4 - core)

    loads = [
        pltpu.make_async_copy(src, dst, lsem.at[n])
        for n, (src, dst) in enumerate(
            (
                (k_hbm, k_in), (v_hbm, v_in), (q_hbm, q_in), (d_hbm, d_in), (o_hbm, o_in),
                (ln_hbm, ln_in), (hid_hbm, hid),
                (wk.at[pl.ds(pl.multiple_of(tp * FEAT, FEAT), FEAT), :], wbuf.at[tp, 0]),
                (wv.at[pl.ds(pl.multiple_of(tp * FEAT, FEAT), FEAT), :], wbuf.at[tp, 1]),
            )
        )
    ]
    for load in loads:
        load.start()

    barrier = pltpu.get_barrier_semaphore()
    for dev in (ypart, mate):
        pl.semaphore_signal(barrier, inc=1, device_id={"ctx": dev}, device_id_type=MESH)
    for step in range(1, NZ):
        dev = ctx_of(y, z_at(step), core)
        pl.semaphore_signal(barrier, inc=1, device_id={"ctx": dev}, device_id_type=MESH)
        peer = (tp + step) % TP
        pl.semaphore_signal(barrier, inc=1, device_id={"tp": peer}, device_id_type=MESH)
        if step % 2:
            pl.semaphore_signal(
                barrier, inc=1, device_id={"ctx": ypart, "tp": peer}, device_id_type=MESH
            )

    flip8 = jnp.full((8, 128), order[2 * i], jnp.int32) != jnp.full((8, 128), i, jnp.int32)
    flip_wide = jnp.concatenate([jnp.where(flip8, 1.0, 0.0)] * 16, axis=0)
    flip16 = flip_wide.astype(BF) > 0.5

    def canon(first, second, hl):
        return jnp.where(flip16, second, first) if hl == 0 else jnp.where(flip16, first, second)

    loads[0].wait()
    loads[1].wait()
    for hl in range(2):
        kv[y, z, 2 * hl] = canon(k_in[:SPAN, :], k_in[SPAN:, :], hl)
        kv[y, z, 2 * hl + 1] = canon(v_in[:SPAN, :], v_in[SPAN:, :], hl)
    pl.semaphore_wait(barrier, 2 * NZ + TP // 2)

    def hop(up, d):
        block = kv.at[y, z_at(-d if up else d)]
        return remote(
            block, block, zsend.at[up, d], zrecv.at[up, d + 1], ctx=up_dev if up else down_dev
        )

    def across(zz, act):
        @pl.when(y == 0)
        def _():
            block = kv.at[0, zz, 0:2]
            act(remote(block, block, ysend.at[zz], yrecv.at[zz], ctx=ypart))

        @pl.when(y == 1)
        def _():
            block = kv.at[1, zz]
            act(remote(block, block, ysend.at[zz], yrecv.at[zz], ctx=ypart))

    def across_wait(zz):
        @pl.when(y == 1)
        def _():
            block = kv.at[0, zz, 0:2]
            remote(block, block, ysend.at[zz], yrecv.at[zz], ctx=ypart).wait_recv()

        @pl.when(y == 0)
        def _():
            block = kv.at[1, zz]
            remote(block, block, ysend.at[zz], yrecv.at[zz], ctx=ypart).wait_recv()

    hop(1, 0).start()
    hop(0, 0).start()
    across(z, lambda copy: copy.start())

    for load in loads[2:6]:
        load.wait()
    for hl in range(2):
        for h in range(8):
            cols = slice(h * 128, (h + 1) * 128)
            for full, here in ((qb, q_in), (db, d_in)):
                full[core, hl, cols, :] = canon(here[:SPAN, cols], here[SPAN:, cols], hl)
            ob[hl, cols, :] = canon(o_in[:SPAN, cols], o_in[SPAN:, cols], hl)
    swaps = [
        remote(ref.at[core], ref.at[core], xsend.at[n], xrecv.at[n], ctx=mate)
        for n, ref in enumerate((qb, db, terms))
    ]
    swaps[0].start()
    swaps[1].start()
    both = ln_in[...] * LOG2E
    terms[core, 0, 0] = jnp.where(flip8, both[:, SPAN:], both[:, :SPAN])
    terms[core, 1, 0] = jnp.where(flip8, both[:, :SPAN], both[:, SPAN:])
    ones = jnp.ones((16, 128), BF)
    head = lax.broadcasted_iota(jnp.int32, (8, 128), 0)
    for hl in range(2):
        prod = db[core, hl].astype(F32) * ob[hl].astype(F32)
        high = prod.astype(BF)
        low = (prod - high.astype(F32)).astype(BF)
        flat = (dot(ones, high, NT) + dot(ones, low, NT))[:8, :]
        delta = flat[:, 0:128]
        for h in range(1, 8):
            delta = jnp.where(head == h, flat[:, h * 128 : (h + 1) * 128], delta)
        terms[core, hl, 1] = delta
    swaps[2].start()

    def zero(n, _):
        for at in range(4):
            acc[n // NZ, n % NZ, at] = jnp.zeros((128, 128), F32)
        return 0

    lax.fori_loop(0, 2 * NZ, zero, 0)
    dqa[...] = jnp.zeros_like(dqa)

    head_of = lax.broadcasted_iota(jnp.int32, (32, 1024), 1) // 128
    pick = (lax.broadcasted_iota(jnp.int32, (32, 1024), 0) % 8 == head_of).astype(F32).astype(BF)

    def row_terms(slot):
        for hl in range(2):
            for at, wide_ref in ((0, lnb), (1, deb)):
                term = terms[slot, hl, at]
                p1 = term.astype(BF)
                rest = term - p1.astype(F32)
                p2 = rest.astype(BF)
                rest = rest - p2.astype(F32)
                p3 = rest.astype(BF)
                parts = jnp.concatenate(
                    [p1.astype(F32), p2.astype(F32), p3.astype(F32), jnp.zeros((8, 128), F32)],
                    axis=0,
                ).astype(BF)
                wide = dot(parts, pick, TN)
                for h in range(8):
                    cols = slice(h * 128, (h + 1) * 128)
                    wide_ref[slot, hl, cols, :] = wide[:, cols]

    row_terms(core)

    def pump(d):
        for up in (1, 0):

            @pl.when(d <= reach[up])
            def _():
                hop(up, d - 1).wait_recv()

                @pl.when(d < reach[up])
                def _():
                    hop(up, d).start()

                across(z_at(-d if up else d), lambda copy: copy.start())

    pump(1)
    for swap in swaps:
        swap.wait()
    row_terms(other)

    def unit(yp, w, hk, hq, masked):
        ra = 2 * w
        rb = 2 * w + 1
        k = jnp.concatenate([kv[yp, ra, 2 * hk], kv[yp, rb, 2 * hk]], axis=0)
        v = jnp.concatenate([kv[yp, ra, 2 * hk + 1], kv[yp, rb, 2 * hk + 1]], axis=0)
        gk = None
        gv = None
        for slot in range(2):
            q = qb[slot, hq]
            d = db[slot, hq]
            ln = lnb[slot, hq]
            de = deb[slot, hq]
            scores = dot(q, k, NT)
            dp = dot(d, v, NT)
            prob = jnp.exp2(scores * (SCALE * LOG2E) - jnp.concatenate([ln, ln], axis=1))
            if masked:
                qi = 2 * chip + slot
                qspan = jnp.where(hq == 0, qi, 63 - qi)
                shape = (1024, 128)
                gap = (
                    lax.broadcasted_iota(jnp.int32, shape, 0) % SPAN
                    - lax.broadcasted_iota(jnp.int32, shape, 1)
                )
                seen = []
                for rk in (ra, rb):
                    ki = 2 * (yp * NZ + rk) + core
                    kspan = jnp.where(hk == 0, ki, 63 - ki)
                    seen.append(gap >= (kspan - qspan) * SPAN)
                prob = jnp.concatenate(
                    [
                        jnp.where(seen[0], prob[:, :128], 0.0),
                        jnp.where(seen[1], prob[:, 128:], 0.0),
                    ],
                    axis=1,
                )
            ds = (prob * (dp - jnp.concatenate([de, de], axis=1))).astype(BF)
            pr = prob.astype(BF)
            dqa[slot, hq] += mm(ds, k)
            gk = dot(q, ds, TN) if gk is None else gk + dot(q, ds, TN)
            gv = dot(d, pr, TN) if gv is None else gv + dot(d, pr, TN)
        acc[yp, ra, 2 * hk] += gk[:, :128]
        acc[yp, rb, 2 * hk] += gk[:, 128:]
        acc[yp, ra, 2 * hk + 1] += gv[:, :128]
        acc[yp, rb, 2 * hk + 1] += gv[:, 128:]

    def pair_at(n):
        side = jnp.where(n == 1, 2 * odd - 1, 1 - 2 * odd)
        return (quad + jnp.where(n == 0, 0, jnp.where(n == 2, 2, side)) + 4) % 4

    def half(ref, p):
        return ref.at[2 * p : 2 * p + 2]

    def sum_y(zz, p):
        return remote(
            half(ysum_out.at[zz], p), half(ysum_in.at[zz], p),
            ysem_s.at[zz, p], ysem_r.at[zz, p], ctx=ypart,
        )

    def sum_across(zz, act):
        act(sum_y(zz, 0))

        @pl.when(y == 0)
        def _():
            act(sum_y(zz, 1))

    def way(zz):
        ahead = (zz - z + NZ) % NZ
        up = (ahead <= reach[1]).astype(jnp.int32)
        return up, jnp.where(up == 1, ahead, NZ - ahead)

    def sum_hop(zz, up, at, p):
        return remote(
            half(sum_out.at[zz], p), half(sum_in.at[up, at], p),
            ssend.at[zz, p], srecv.at[up, at, p],
            ctx=jnp.where(up == 1, up_dev, down_dev),
        )

    def sum_home(zz, up, at, p):
        return remote(
            half(sum_out.at[zz], p), half(home_in.at[up, at], p),
            ssend.at[zz, p], homer.at[up, at, p], ctx=ctx_of(y, zz, core),
        )

    def merge(zz, up, a, p):
        limit = jnp.where(up == 1, reach[1], reach[0])
        at = slice(2 * p, 2 * p + 2)

        @pl.when(a < limit)
        def _():
            sum_hop(zz, up, a, p).wait_recv()
            sum_out[zz, at] = (acc[y, zz, at] + sum_in[up, a, at].astype(F32)).astype(BF)

        @pl.when(a == limit)
        def _():
            sum_out[zz, at] = acc[y, zz, at].astype(BF)

    def pass_far(zz):
        up, a = way(zz)
        for p in range(2):
            add_half(zz, p)
            merge(zz, up, a, p)
            sum_hop(zz, up, a - 1, p).start()

    def pass_mid(zz):
        up, a = way(zz)
        for p in range(2):
            add_half(zz, p)
            merge(zz, up, a, p)
            sum_home(zz, up, a, p).start()

    def pass_near(zz):
        up, a = way(zz)
        for p in range(2):
            add_half(zz, p)
            at = slice(2 * p, 2 * p + 2)
            sum_out[zz, at] = acc[y, zz, at].astype(BF)
            sum_home(zz, up, a, p).start()

    def send_across(n):
        for zz in far_near(n):
            ysum_out[zz] = acc[1 - y, zz].astype(BF)
            sum_across(zz, lambda copy: copy.start())

    def add_half(zz, p):
        def add():
            sum_y(zz, p).wait_recv()
            at = slice(2 * p, 2 * p + 2)
            acc[y, zz, at] += ysum_in[zz, at].astype(F32)

        if p == 0:
            add()
        else:
            pl.when(y == 1)(add)

    def add_across(zz):
        add_half(zz, 0)
        add_half(zz, 1)

    def far_near(n):
        w = pair_at(n)
        first = 2 * w
        _, da = way(first)
        _, db = way(first + 1)
        flip = (da < db).astype(jnp.int32)
        return first + flip, first + 1 - flip

    def weight_copies(step):
        peer = (tp + step) % TP
        out = []
        for n, ref in enumerate((wk, wv)):
            rows = pl.ds(pl.multiple_of(peer * FEAT + core * HALF_FEAT, 64), HALF_FEAT)
            mine = pl.ds(pl.multiple_of(core * HALF_FEAT, 64), HALF_FEAT)
            out.append(
                remote(
                    ref.at[rows, :], wbuf.at[tp, n, mine, :],
                    wsend.at[step, n], wrecv.at[step, n], tp=peer, ctx=jnp.where(step % 2 == 1, ypart, i),
                )
            )
        return out

    def weight_forwards(step):
        giver = (tp + TP - step) % TP
        out = []
        for n in range(2):
            mine = pl.ds(pl.multiple_of(core * HALF_FEAT, 64), HALF_FEAT)
            block = wbuf.at[giver, n, mine, :]
            out.append(remote(block, block, fsend.at[step, n], frecv.at[step, n], ctx=mate))
        return out

    def half_step(x, _):
        n = x // 2
        w = pair_at(n)
        far = jnp.where(x < 6, x % 2, 1 - x % 2)
        yp = (y + far) % 2

        @pl.when(far == 1)
        def _():
            across_wait(2 * w)
            across_wait(2 * w + 1)

        @pl.when(x < 7)
        def _():
            for copy in weight_copies(x + 1):
                copy.start()

        unit(yp, w, 0, 1, False)

        for at, d in ((0, 2), (3, 4)):

            @pl.when(x == at)
            def _():
                pump(d)

        @pl.when(x == 7)
        def _():
            further, _ = far_near(2)
            pass_far(further)

        own = jnp.logical_and(far == 0, n == 0)

        @pl.when(own)
        def _():
            def masked_unit(hl, _):
                unit(yp, w, hl, hl, True)
                return 0

            lax.fori_loop(0, 2, masked_unit, 0)

        @pl.when(jnp.logical_not(own))
        def _():
            hl = jnp.where(yp * NZ + 2 * w < chip, 0, 1)
            unit(yp, w, hl, hl, False)

        @pl.when(far == 1)
        def _():
            send_across(n)

        @pl.when(x == 1)
        def _():
            pump(3)

        @pl.when(x == 3)
        def _():
            add_across(z)
            pass_near(2 * quad + 1 - odd)

        @pl.when(x == 5)
        def _():
            for zz in far_near(1):
                pass_near(zz)

        @pl.when(x > 1)
        def _():
            for copy in weight_copies(x - 1):
                copy.wait_recv()
            for copy in weight_forwards(x - 1):
                copy.start()

        return 0

    lax.fori_loop(0, 8, half_step, 0)

    _, nearer = far_near(2)
    pass_far(nearer)
    dqs[...] = (dqa[other] * SCALE).astype(BF)
    dq_copy = remote(dqs, dqr, dsem.at[0], dsem.at[1], ctx=mate)
    dq_copy.start()
    for copy in weight_copies(TP - 1):
        copy.wait_recv()
    for copy in weight_forwards(TP - 1):
        copy.start()
    for zz in far_near(3):
        pass_mid(zz)
    dq_copy.wait()
    for h in range(8):
        cols = slice(h * 128, (h + 1) * 128)
        low = (dqa[core, 0, cols, :] * SCALE + dqr[0, cols, :].astype(F32)).astype(BF)
        high = (dqa[core, 1, cols, :] * SCALE + dqr[1, cols, :].astype(F32)).astype(BF)
        dq_out[0:SPAN, cols] = jnp.where(flip16, high, low)
        dq_out[SPAN:, cols] = jnp.where(flip16, low, high)

    def take(up, a):
        for p in range(2):
            sum_home(z, up, a, p).wait_recv()
        acc[y, z] += home_in[up, a].astype(F32)

    for up, a in ((0, 1), (1, 1), (0, 2), (1, 2), (odd, 3)):
        take(up, a)
    for out, at, factor in ((dk_out, 0, SCALE), (dv_out, 1, 1.0)):
        low = (acc[y, z, at] * factor).T.astype(BF)
        high = (acc[y, z, at + 2] * factor).T.astype(BF)
        cols = slice(at * 128, (at + 1) * 128)
        for rows, value in (
            (slice(0, SPAN), jnp.where(flip16, high, low)),
            (slice(SPAN, 2 * SPAN), jnp.where(flip16, low, high)),
        ):
            out[rows, :] = value
            dkv[rows, cols] = value

    def spread(step):
        return remote(dkv, gathered.at[tp], tsend.at[step], trecv.at[step], tp=(tp + step) % TP)

    for step in range(1, TP):
        spread(step).start()

    mine = dkv[...]
    loads[6].wait()

    def rows_of(yp, zz, k):
        return pl.ds(pl.multiple_of(((yp * NZ + zz) * 2 + k) * WROWS, 32), WROWS)

    def swap_part(yp):
        return remote(cs.at[yp], cr.at[yp], csend.at[yp], crecv.at[yp], ctx=mate)

    for turn in range(2):
        yp = (1 - y) if turn == 0 else y
        for n in range(5):
            at = pl.ds(pl.multiple_of(yp * 2560 + n * 512, 512), 512)
            part[at, :] = dot(hid[:, at], mine, TN)

        def fill(zz, _):
            cs[yp, zz] = part[rows_of(yp, zz, other), :].astype(BF)
            return 0

        lax.fori_loop(0, NZ, fill, 0)
        swap_part(yp).start()
    def own_part(yp, zz, ch):
        cols = slice(ch * 128, (ch + 1) * 128)
        return part[rows_of(yp, zz, core), cols] + cr[yp, zz, :, cols].astype(F32)

    def arm(up, a, q):
        return remote(
            gout.at[up, a, q], gin.at[up, a - 1, q],
            gsend.at[up, a, q], grecv.at[up, a - 1, q],
            ctx=up_dev if up else down_dev,
        )

    def arms(k, _):
        a = 4 - k
        for turn in range(2):
            yp = (1 - y) if turn == 0 else y

            @pl.when(k == 0)
            def _():
                swap_part(yp).wait()

            for ch in range(2):
                q = yp * 2 + ch
                for up in (1, 0):
                    zz = (z + a) % NZ if up else (z - a + NZ) % NZ

                    @pl.when(a == reach[up])
                    def _():
                        gout[up, a, q] = own_part(yp, zz, ch).astype(BF)

                    @pl.when(a < reach[up])
                    def _():
                        arm(up, a + 1, q).wait_recv()
                        mix = own_part(yp, zz, ch) + gin[up, a, q].astype(F32)
                        gout[up, a, q] = mix.astype(BF)

                    @pl.when(a <= reach[up])
                    def _():
                        arm(up, a, q).start()

        return 0

    lax.fori_loop(0, 4, arms, 0)

    def plane_sum(yp, ch):
        q = yp * 2 + ch
        arm(1, 1, q).wait_recv()
        arm(0, 1, q).wait_recv()
        return own_part(yp, z, ch) + gin[1, 0, q].astype(F32) + gin[0, 0, q].astype(F32)

    f_copies = []
    for ch in range(2):
        fs[ch] = plane_sum(1 - y, ch).astype(BF)
        f_copies.append(
            remote(fs.at[ch], fr.at[ch], dsem.at[2 + 2 * ch], dsem.at[3 + 2 * ch], ctx=ypart)
        )
        f_copies[ch].start()

    gathered[tp] = mine
    loads[7].wait()
    loads[8].wait()
    for step in range(1, TP):
        for copy in weight_forwards(step):
            copy.wait()
        spread(step).wait_recv()
    total = None
    for giver in range(TP):
        got = gathered[giver]
        term = dot(got[:, :128], wbuf[giver, 0], NT) + dot(got[:, 128:], wbuf[giver, 1], NT)
        total = term if total is None else total + term
    dh_out[...] = total.astype(BF)

    for ch, out in ((0, gk_out), (1, gv_out)):
        mine_sum = plane_sum(y, ch)
        f_copies[ch].wait()
        out[...] = mine_sum + fr[ch].astype(F32)

    def drain(s, _):
        across(s, lambda copy: copy.wait_send())
        sum_across(s, lambda copy: copy.wait_send())

        @pl.when(s > 0)
        def _():
            for copy in weight_copies(s):
                copy.wait_send()
            for p in range(2):
                sum_hop(z_at(s), 0, 0, p).wait_send()
            spread(s).wait_send()

        for up in (0, 1):

            @pl.when(s < reach[up])
            def _():
                hop(up, s).wait_send()
                for q in range(4):
                    arm(up, s + 1, q).wait_send()

        return 0

    lax.fori_loop(0, NZ, drain, 0)


def backward(*args):
    vmem = pl.BlockSpec(memory_space=pltpu.VMEM)
    hbm = pl.BlockSpec(memory_space=pl.ANY)
    dma = pltpu.SemaphoreType.DMA
    sds = jax.ShapeDtypeStruct
    rows = (2, 2, 1024, 128)
    block = (4, 128, 128)
    piece = (WROWS, 256)
    return pl.pallas_call(
        kernel,
        out_shape=[
            sds((256, 1024), BF),
            sds((256, 128), BF),
            sds((256, 128), BF),
            sds((WROWS, 128), F32),
            sds((WROWS, 128), F32),
            sds((256, FEAT), BF),
        ],
        in_specs=[pl.BlockSpec(memory_space=pltpu.SMEM)] + [hbm] * 9,
        out_specs=[vmem] * 6,
        scratch_shapes=[
            pltpu.VMEM((256, 1024), BF),
            pltpu.VMEM((256, 128), BF),
            pltpu.VMEM((256, 128), BF),
            pltpu.VMEM((256, 1024), BF),
            pltpu.VMEM((256, 1024), BF),
            pltpu.VMEM((8, 256), F32),
            pltpu.VMEM((256, 5120), BF),
            pltpu.VMEM(rows, BF),
            pltpu.VMEM(rows, BF),
            pltpu.VMEM((2, 1024, 128), BF),
            pltpu.VMEM((2, 2, 2, 8, 128), F32),
            pltpu.VMEM(rows, F32),
            pltpu.VMEM(rows, F32),
            pltpu.VMEM(rows, F32),
            pltpu.VMEM((2, NZ) + block, BF),
            pltpu.VMEM((2, NZ) + block, F32),
            pltpu.VMEM((NZ,) + block, BF),
            pltpu.VMEM((NZ,) + block, BF),
            pltpu.VMEM((NZ,) + block, BF),
            pltpu.VMEM((2, 4) + block, BF),
            pltpu.VMEM((2, 4) + block, BF),
            pltpu.VMEM((2, 1024, 128), BF),
            pltpu.VMEM((2, 1024, 128), BF),
            pltpu.VMEM((TP, 2, FEAT, 128), BF),
            pltpu.VMEM((256, 256), BF),
            pltpu.VMEM((TP, 256, 256), BF),
            pltpu.VMEM((5120, 256), F32),
            pltpu.VMEM((2, NZ) + piece, BF),
            pltpu.VMEM((2, NZ) + piece, BF),
            pltpu.VMEM((2, 5, 4, WROWS, 128), BF),
            pltpu.VMEM((2, 4, 4, WROWS, 128), BF),
            pltpu.VMEM((2, WROWS, 128), BF),
            pltpu.VMEM((2, WROWS, 128), BF),
            dma((9,)),
            dma((4,)),
            dma((4,)),
            dma((2, 5)),
            dma((2, 5)),
            dma((NZ,)),
            dma((NZ,)),
            dma((NZ, 2)),
            dma((NZ, 2)),
            dma((NZ, 2)),
            dma((2, 4, 2)),
            dma((2, 4, 2)),
            dma((TP, 2)),
            dma((TP, 2)),
            dma((TP, 2)),
            dma((TP, 2)),
            dma((6,)),
            dma((TP,)),
            dma((TP,)),
            dma((2,)),
            dma((2,)),
            dma((2, 5, 4)),
            dma((2, 5, 4)),
        ],
        compiler_params=pltpu.CompilerParams(
            collective_id=0, has_side_effects=True, vmem_limit_bytes=58 * 2**20
        ),
        cost_estimate=pl.CostEstimate(
            flops=12 * 10**9, bytes_accessed=10**7, transcendentals=9 * 10**6
        ),
    )(*args)


def copy_kernel(*refs):
    sems = refs[18]
    inward = [pltpu.make_async_copy(refs[n], refs[12 + n], sems.at[0, n]) for n in range(6)]
    outward = [pltpu.make_async_copy(refs[12 + n], refs[6 + n], sems.at[1, n]) for n in range(6)]
    for copy in inward:
        copy.start()
    for n in range(6):
        inward[n].wait()
        outward[n].start()
    for copy in outward:
        copy.wait()


def place_outputs(*outs):
    hbm = pl.BlockSpec(memory_space=pl.ANY)
    return pl.pallas_call(
        copy_kernel,
        out_shape=[jax.ShapeDtypeStruct(a.shape, a.dtype) for a in outs],
        in_specs=[hbm] * 6,
        out_specs=[hbm] * 6,
        scratch_shapes=[pltpu.VMEM(a.shape, a.dtype) for a in outs]
        + [pltpu.SemaphoreType.DMA((2, 6))],
        compiler_params=pltpu.CompilerParams(vmem_limit_bytes=60 * 2**20),
    )(*outs)


def shards(q, k, v, o, d, ln, order, hidden, wk, wv):
    return tuple(place_outputs(*backward(order, q, k, v, o, d, ln, hidden, wk, wv)))


def solution(mesh):
    split = P("ctx", "tp")
    in_specs = (split,) * 5 + (P("tp", "ctx"), P(), P("ctx", None), P(None, "tp"), P(None, "tp"))
    return jax.shard_map(
        shards, mesh=mesh, in_specs=in_specs, out_specs=(split,) * 6, check_vma=False
    )
```
